32 devices in a mesh: expert: 8 (over z, y), dp: 4 (over x, core).
Axes of the slice: x: 2, y: 2, z: 4, core: 2. Of those that a mesh axis runs over, the one named last changes fastest.
Arguments:
- tokens: bfloat16 [4096, 3584], P(('expert', 'dp')), may hold values from -6 to 6
- out_grad: bfloat16 [4096, 3584], P(('expert', 'dp')), may hold values from -2 to 2
- expert_ids: int32 [4096, 8], P(('expert', 'dp')), may hold values from 0 to 63, as said below
- route_weights: bfloat16 [4096, 8], P(('expert', 'dp')), may hold values from 0.099609375 to 1
- w_gate: bfloat16 [8, 3584, 1024], P('expert', None, 'dp'), may hold values from -0.09375 to 0.09375
- w_up: bfloat16 [8, 3584, 1024], P('expert', None, 'dp'), may hold values from -0.09375 to 0.09375
- w_down: bfloat16 [8, 1024, 3584], P('expert', 'dp'), may hold values from -0.1875 to 0.1875
Outputs:
- grad_tokens: bfloat16 [4096, 3584], P(('expert', 'dp'))
- grad_route: bfloat16 [4096, 8], P(('expert', 'dp'))
- grad_gate: bfloat16 [8, 3584, 1024], P('expert', None, 'dp')
- grad_upproj: bfloat16 [8, 3584, 1024], P('expert', None, 'dp')
- grad_down: bfloat16 [8, 1024, 3584], P('expert', 'dp')
The draws below stay inside these ranges and needn't reach their ends.
Inputs may be any that keep to these rules, and one draw needn't show every extreme that they name: `expert_ids`: each token's 8 ids are distinct. Ids below 8 are the window's experts. Within the 128 tokens of one device no id below 8 appears more than 20 times.
All inputs are finite; a program needn't handle non-finite values.
Results may differ from the reference program's by a relative error of at most 0.015.
Values may be sent and summed in bfloat16 or wider, within the bound.
No kernel may reach another device: no remote copies, remote signals or barrier semaphores. Data moves between devices by JAX's collectives and lax.ppermute only.
A program may use at most 128 MiB of HBM per device.

```python
import math
import jax
import jax.numpy as jnp
from jax import lax

D = 3584
FF = 1024
TOPK = 8
TOK_DEV = 128
EXPERTS = 8
ALL_EXPERTS = 64
CAP = 20
GROUPS = 4
FF_DEV = 256
TOKENS = 4096


def draw_expert_ids(key, part):
    block_count = TOKENS // TOK_DEV
    route_slots = TOK_DEV * TOPK
    key_hot, key_window, key_shuffle, key_routes = jax.random.split(jax.random.fold_in(key, 11), 4)
    hot_experts = jax.random.permutation(key_hot, EXPERTS)[:2]
    is_hot = jnp.any(jnp.arange(EXPERTS)[:, None] == hot_experts[None, :], axis=1)
    upper_count = 3 * CAP // 5 + 1
    window_counts = jax.random.randint(key_window, (block_count, EXPERTS), 1, upper_count + 1)
    window_counts = jnp.minimum(window_counts, upper_count)
    window_counts = jnp.where(is_hot[None, :], CAP, window_counts)
    remainder = route_slots - jnp.sum(window_counts, axis=1)
    others = ALL_EXPERTS - EXPERTS
    other_index = jnp.arange(others)
    other_counts = remainder[:, None] // others + (other_index[None, :] < remainder[:, None] % others).astype(jnp.int32)
    counts = jnp.concatenate([window_counts, other_counts], axis=1)
    cumulative = jnp.cumsum(counts, axis=1)
    position = jnp.arange(route_slots)
    route_ids = jax.vmap(lambda bounds: jnp.searchsorted(bounds, position, side='right'))(cumulative)
    route_ids = route_ids.reshape(block_count, TOPK, TOK_DEV).transpose(0, 2, 1)
    block_keys = jax.random.split(key_shuffle, block_count)
    shuffle = jax.vmap(lambda one_key: jax.random.permutation(one_key, TOK_DEV))(block_keys)
    route_ids = jnp.take_along_axis(route_ids, shuffle[:, :, None], axis=1)
    scores = jax.random.randint(key_routes, (block_count, TOK_DEV, TOPK), 0, 1000) * TOPK + jnp.arange(TOPK)[None, None, :]
    route_order = jnp.argsort(scores, axis=2)
    route_ids = jnp.take_along_axis(route_ids, route_order, axis=2)
    return route_ids.reshape(TOKENS, TOPK).astype(jnp.int32)


def level_of(stream_key, shape, pieces, least, largest):
    factor_of = 1.0
    for dim, parts in pieces:
        draws = jax.random.uniform(jax.random.fold_in(jax.random.fold_in(stream_key, 6), dim), (parts,), jnp.float32, least / len(pieces), largest / len(pieces))
        factor_of = factor_of * jnp.repeat(jnp.exp(draws), shape[dim] // parts).reshape((-1,) + (1,) * (len(shape) - 1 - dim))
    return factor_of


def centred(own_key, shape, width, reach, cuts=(), held_as=jnp.bfloat16):
    entries = jax.random.normal(own_key, shape, jnp.float32) * width
    if len(cuts) > 0:
        entries = level_of(own_key, shape, cuts, -0.22, 0.18) * entries
    return jnp.clip(entries, min=-reach, max=reach).astype(held_as)


def setup_inputs(seed: int = 0) -> dict:
    key_of = jax.random.split(jax.random.key(seed), 8)
    return {
        "tokens": centred(key_of[0], (TOKENS, D), 1.0, 6.0, ((0, 32),)),
        "out_grad": centred(key_of[1], (TOKENS, D), 0.3, 2.0, ((0, 32),)),
        "expert_ids": draw_expert_ids(jax.random.fold_in(key_of[7], 71), 0),
        "route_weights": jnp.clip(jnp.exp(math.log(1.0) - 2.306499 * jax.random.uniform(key_of[3], (TOKENS, TOPK), jnp.float32) ** level_of(key_of[3], (TOKENS, TOPK), ((0, 32),), -0.2, 0.2)), 0.099609375, 1.0).astype(jnp.bfloat16),
        "w_gate": centred(key_of[4], (EXPERTS, D, FF), D ** -0.5, 0.09375, ((0, 8), (2, 4))),
        "w_up": centred(key_of[5], (EXPERTS, D, FF), D ** -0.5, 0.09375, ((0, 8), (2, 4))),
        "w_down": centred(key_of[6], (EXPERTS, FF, D), FF ** -0.5, 0.1875, ((0, 8), (1, 4))),
    }


def rounded_back(values):
    return lax.optimization_barrier(values.astype(jnp.bfloat16)).astype(jnp.float32)


def reference(tokens, out_grad, expert_ids, route_weights, w_gate, w_up, w_down):
    block_count = TOKENS // TOK_DEV
    route_slots = TOK_DEV * TOPK
    flat_ids = expert_ids.reshape(block_count, route_slots)
    onehot = (flat_ids[:, :, None] == jnp.arange(EXPERTS, dtype=jnp.int32)[None, None, :]).astype(jnp.int32)
    ranking = jnp.sum((jnp.cumsum(onehot, axis=1) - 1) * onehot, axis=2)
    target = jnp.where(flat_ids < EXPERTS, flat_ids * CAP + ranking, EXPERTS * CAP).astype(jnp.int32)
    local_index = jnp.arange(route_slots, dtype=jnp.int32)

    def fill_slots(dest):
        return jnp.full((EXPERTS * CAP,), -1, jnp.int32).at[dest].set(local_index, mode="drop")

    slot_table = jax.vmap(fill_slots)(target)
    offsets = (jnp.arange(block_count, dtype=jnp.int32) * route_slots)[:, None]
    global_table = jnp.where(slot_table >= 0, slot_table + offsets, -1)
    per_expert = global_table.reshape(block_count, EXPERTS, CAP).transpose(1, 0, 2).reshape(EXPERTS, block_count * CAP)
    flat_weights = route_weights.reshape(-1).astype(jnp.float32)

    def one_expert(carry, inputs):
        grad_sum, route_sum = carry
        slot_index, gate_w, up_w, down_w = inputs
        occupied = slot_index >= 0
        clamped = jnp.where(occupied, slot_index, 0)
        owner_token = clamped // TOPK
        x_rows = tokens[owner_token]
        dy_rows = out_grad[owner_token]
        weight = jnp.where(occupied, flat_weights[clamped], 0.0)[:, None]
        gate_value = jnp.dot(x_rows, gate_w, preferred_element_type=jnp.float32)
        up_value = jnp.dot(x_rows, up_w, preferred_element_type=jnp.float32)
        sigmoid_gate = jax.nn.sigmoid(gate_value)
        hidden = (gate_value * sigmoid_gate * up_value).astype(jnp.bfloat16)
        back_proj = lax.dot_general(dy_rows, down_w, (((1,), (1,)), ((), ())), preferred_element_type=jnp.float32)
        row_count = x_rows.shape[0]
        hidden_f = hidden.astype(jnp.float32)
        group_route = jnp.sum((hidden_f * back_proj).reshape(row_count, GROUPS, FF_DEV), axis=2)
        route_value = jnp.sum(rounded_back(group_route), axis=1).astype(jnp.bfloat16)
        scaled = weight * back_proj
        d_gate = (scaled * up_value * sigmoid_gate * (1.0 + gate_value * (1.0 - sigmoid_gate))).astype(jnp.bfloat16)
        d_up = (scaled * gate_value * sigmoid_gate).astype(jnp.bfloat16)
        weighted = (weight * hidden_f).astype(jnp.bfloat16)
        contract_rows = (((0,), (0,)), ((), ()))
        grad_g = lax.dot_general(x_rows, d_gate, contract_rows, preferred_element_type=jnp.float32).astype(jnp.bfloat16)
        grad_u = lax.dot_general(x_rows, d_up, contract_rows, preferred_element_type=jnp.float32).astype(jnp.bfloat16)
        grad_d = lax.dot_general(weighted, dy_rows, contract_rows, preferred_element_type=jnp.float32).astype(jnp.bfloat16)
        gate_groups = gate_w.astype(jnp.float32).reshape(D, GROUPS, FF_DEV)
        up_groups = up_w.astype(jnp.float32).reshape(D, GROUPS, FF_DEV)
        dg_groups = d_gate.astype(jnp.float32).reshape(row_count, GROUPS, FF_DEV)
        du_groups = d_up.astype(jnp.float32).reshape(row_count, GROUPS, FF_DEV)
        group_part = jnp.einsum("rqf,dqf->rqd", dg_groups, gate_groups) + jnp.einsum("rqf,dqf->rqd", du_groups, up_groups)
        contrib = jnp.sum(rounded_back(group_part), axis=1)
        contrib_f = rounded_back(contrib)
        token_target = jnp.where(occupied, owner_token, TOKENS)
        grad_sum = grad_sum.at[token_target].add(contrib_f, mode="drop")
        route_target = jnp.where(occupied, clamped, TOKENS * TOPK)
        route_sum = route_sum.at[route_target].set(route_value.astype(jnp.float32), mode="drop")
        return (grad_sum, route_sum), (grad_g, grad_u, grad_d)

    start = (jnp.zeros((TOKENS, D), jnp.float32), jnp.zeros((TOKENS * TOPK,), jnp.float32))
    (grad_sum, route_sum), (grad_gate, grad_upproj, grad_down) = lax.scan(one_expert, start, (per_expert, w_gate, w_up, w_down))
    return (grad_sum.astype(jnp.bfloat16), route_sum.reshape(TOKENS, TOPK).astype(jnp.bfloat16), grad_gate, grad_upproj, grad_down)
```

```python
import functools

import jax
import jax.numpy as jnp
from jax import lax
from jax.experimental import pallas as pl
from jax.experimental.pallas import tpu as pltpu
from jax.sharding import PartitionSpec as P

AXES = ("expert", "dp")
VMEM_LIMIT = 56 * 1024 * 1024
EXTRA = 128


def vmem():
    return pl.BlockSpec(memory_space=pltpu.VMEM)


def smem():
    return pl.BlockSpec(memory_space=pltpu.SMEM)


def params():
    return pltpu.CompilerParams(vmem_limit_bytes=VMEM_LIMIT)


def cost(flops, size):
    return pl.CostEstimate(flops=int(flops), bytes_accessed=int(size), transcendentals=0)


def chunks(total, step):
    return [(start, min(step, total - start)) for start in range(0, total, step)]


def routed(me, ids, lanes):
    target = lax.broadcasted_iota(jnp.int32, (1, lanes), 1) ^ me
    return [ids[:, k : k + 1] == target for k in range(ids.shape[1])]


def pick_kernel(expert_count, capacity, me_ref, ids_ref, weight_ref, tok_ref, grad_ref, *outs):
    rows, width = tok_ref.shape
    lanes = 128
    me = me_ref[0]
    ids = ids_ref[...]
    weights = weight_ref[...].astype(jnp.float32)
    hits = routed(me, ids, lanes)
    lane = lax.broadcasted_iota(jnp.int32, (rows, lanes), 1)
    has = jnp.zeros((rows, lanes), jnp.float32)
    weight = jnp.zeros((rows, lanes), jnp.float32)
    for k, hit in enumerate(hits):
        hit = hit & (lane < expert_count)
        has = jnp.where(hit, 1.0, has)
        weight = jnp.where(hit, weights[:, k : k + 1], weight)
    has_t = has.T
    weight_t = weight.T
    before = lax.broadcasted_iota(jnp.int32, (rows, rows), 0) < lax.broadcasted_iota(
        jnp.int32, (rows, rows), 1
    )
    rank_t = jnp.dot(
        has_t.astype(jnp.bfloat16),
        before.astype(jnp.float32).astype(jnp.bfloat16),
        preferred_element_type=jnp.float32,
    )
    slot_t = jnp.where(has_t > 0.0, rank_t, -1.0).astype(jnp.int32)
    index = lax.broadcasted_iota(jnp.int32, (2 * capacity, rows), 0)
    for s in range(expert_count):
        slot = slot_t[s : s + 1, :]
        pick_x = jnp.where((slot >= 0) & (slot == index), 1.0, 0.0).astype(jnp.bfloat16)
        pick_dy = jnp.where(
            (slot >= 0) & (slot + capacity == index), weight_t[s : s + 1, :], 0.0
        ).astype(jnp.bfloat16)
        pick_x = jnp.where(index < capacity, pick_x.astype(jnp.float32), 0.0).astype(jnp.bfloat16)
        for start, size in chunks(width, 896):
            part = slice(start, start + size)
            picked = jnp.dot(pick_x, tok_ref[:, part], preferred_element_type=jnp.float32)
            picked += jnp.dot(pick_dy, grad_ref[:, part], preferred_element_type=jnp.float32)
            outs[s][:, part] = picked.astype(jnp.bfloat16)


def pick_rows(me, ids, weights, tokens, out_grad, expert_count, capacity):
    rows, width = tokens.shape
    block = jax.ShapeDtypeStruct((2 * capacity, width), jnp.bfloat16)
    return pl.pallas_call(
        functools.partial(pick_kernel, expert_count, capacity),
        out_shape=[block] * expert_count,
        in_specs=[smem(), vmem(), vmem(), vmem(), vmem()],
        out_specs=[vmem()] * expert_count,
        compiler_params=params(),
        cost_estimate=cost(1e9, 4e6),
        name="pick_rows",
    )(me, ids, weights, tokens, out_grad)


def compact_kernel(capacity, count, *refs):
    blocks, out_ref = refs[:count], refs[count]
    for i, ref in enumerate(blocks):
        value = ref[...].astype(jnp.float32)
        place = slice(i * capacity, (i + 1) * capacity)
        out_ref[0, place, :] = value[:capacity].astype(jnp.bfloat16)
        out_ref[1, place, :] = value[capacity:].astype(jnp.bfloat16)


def compact(blocks, capacity):
    width = blocks[0].shape[1]
    count = len(blocks)
    return pl.pallas_call(
        functools.partial(compact_kernel, capacity, count),
        out_shape=jax.ShapeDtypeStruct((2, count * capacity, width), jnp.bfloat16),
        in_specs=[vmem()] * count,
        out_specs=vmem(),
        compiler_params=params(),
        cost_estimate=cost(1e6, 8 * count * capacity * width),
        name="compact",
    )(*blocks)


def expert_kernel(
    tiles, own, other, gate_ref, up_ref, down_ref, keep_ref, send_ref, units_ref, gate_w, up_w, total
):
    step = pl.program_id(0)
    rows = own.shape[1]
    hidden_units = gate_ref.shape[1]
    tile = gate_ref.shape[0]

    @pl.when(step == 0)
    def _():
        total[...] = jnp.zeros_like(total)

    @pl.when(step < tiles)
    def _():
        gate_w[step] = gate_ref[...]
        up_w[step] = up_ref[...]
        x = jnp.concatenate([own[0], other[0]], axis=0)
        dy = jnp.concatenate([own[1], other[1]], axis=0)
        total[0] += jnp.dot(x, gate_ref[...], preferred_element_type=jnp.float32)
        total[1] += jnp.dot(x, up_ref[...], preferred_element_type=jnp.float32)
        total[2] += lax.dot_general(
            dy, down_ref[...], (((1,), (1,)), ((), ())), preferred_element_type=jnp.float32
        )

    @pl.when(step == tiles - 1)
    def _():
        gate_value = total[0]
        up_value = total[1]
        back = total[2]
        sigmoid = jax.nn.sigmoid(gate_value)
        silu = gate_value * sigmoid
        hidden = (silu * up_value).astype(jnp.bfloat16)
        d_gate = back * up_value * sigmoid * (1.0 + gate_value * (1.0 - sigmoid))
        units_ref[:, 0:hidden_units] = d_gate.astype(jnp.bfloat16)
        units_ref[:, hidden_units : 2 * hidden_units] = (back * silu).astype(jnp.bfloat16)
        units_ref[:, 2 * hidden_units :] = hidden
        route = jnp.sum(hidden.astype(jnp.float32) * back, axis=1, keepdims=True)
        total[2, :, 0:EXTRA] = jnp.broadcast_to(route, (2 * rows, EXTRA))

    @pl.when((step >= tiles) & (step < 2 * tiles))
    def _():
        at = step - tiles
        contract = (((1,), (1,)), ((), ()))
        part = lax.dot_general(
            units_ref[:, 0:hidden_units], gate_w[at], contract, preferred_element_type=jnp.float32
        )
        part += lax.dot_general(
            units_ref[:, hidden_units : 2 * hidden_units],
            up_w[at],
            contract,
            preferred_element_type=jnp.float32,
        )
        part = part.astype(jnp.bfloat16)
        start = pl.multiple_of(at * tile, 128)
        keep_ref[:, pl.ds(start, tile)] = part[:rows]
        send_ref[:, pl.ds(start, tile)] = part[rows:]

    @pl.when(step == 2 * tiles - 1)
    def _():
        route = total[2, :, 0:EXTRA].astype(jnp.bfloat16)
        width = tiles * tile
        keep_ref[:, width:] = route[:rows]
        send_ref[:, width:] = route[rows:]


def run_expert(own, other, gate, up, down):
    _, rows, width = own.shape
    units = gate.shape[1]
    tile = width // 4 if width % 512 == 0 else width
    tiles = width // tile
    last = tiles - 1
    out = jax.ShapeDtypeStruct((rows, width + EXTRA), jnp.bfloat16)
    return pl.pallas_call(
        functools.partial(expert_kernel, tiles),
        grid=(2 * tiles,),
        out_shape=[out, out, jax.ShapeDtypeStruct((2 * rows, 3 * units), jnp.bfloat16)],
        in_specs=[
            pl.BlockSpec((2, rows, tile), lambda i: (0, 0, jnp.minimum(i, last))),
            pl.BlockSpec((2, rows, tile), lambda i: (0, 0, jnp.minimum(i, last))),
            pl.BlockSpec((tile, units), lambda i: (jnp.minimum(i, last), 0)),
            pl.BlockSpec((tile, units), lambda i: (jnp.minimum(i, last), 0)),
            pl.BlockSpec((units, tile), lambda i: (0, jnp.minimum(i, last))),
        ],
        out_specs=[
            pl.BlockSpec((rows, width + EXTRA), lambda i: (0, 0)),
            pl.BlockSpec((rows, width + EXTRA), lambda i: (0, 0)),
            pl.BlockSpec((2 * rows, 3 * units), lambda i: (0, 0)),
        ],
        scratch_shapes=[
            pltpu.VMEM((tiles, tile, units), jnp.bfloat16),
            pltpu.VMEM((tiles, tile, units), jnp.bfloat16),
            pltpu.VMEM((3, 2 * rows, units), jnp.float32),
        ],
        compiler_params=params(),
        cost_estimate=cost(20 * rows * width * units, 6 * width * units + 12 * rows * width),
        name="run_expert",
    )(own, other, gate, up, down)


def half_kernel(keep_ref, recv_ref, out_ref):
    rows = out_ref.shape[0]
    out_ref[...] = (
        keep_ref[rows:, :].astype(jnp.float32) + recv_ref[rows:, :].astype(jnp.float32)
    ).astype(jnp.bfloat16)


def add_half(keep, recv):
    rows, width = keep.shape
    return pl.pallas_call(
        half_kernel,
        out_shape=jax.ShapeDtypeStruct((rows // 2, width), jnp.bfloat16),
        in_specs=[vmem(), vmem()],
        out_specs=vmem(),
        compiler_params=params(),
        cost_estimate=cost(rows * width, 5 * rows * width),
        name="add_half",
    )(keep, recv)


def finish_kernel(capacity, keep_ref, recv_ref, far_ref, *outs):
    rows = far_ref.shape[0]
    half = (far_ref.shape[1] - EXTRA) // 2

    def summed(part):
        return (
            keep_ref[:rows, part].astype(jnp.float32)
            + recv_ref[:rows, part].astype(jnp.float32)
            + far_ref[:, part].astype(jnp.float32)
        )

    for h in range(2):
        for start, size in chunks(half, 896):
            value = summed(slice(h * half + start, h * half + start + size))
            for i, out in enumerate(outs):
                out[h * capacity : (h + 1) * capacity, start : start + size] = value[
                    i * capacity : (i + 1) * capacity
                ].astype(jnp.bfloat16)
    value = summed(slice(2 * half, 2 * half + EXTRA))
    for i, out in enumerate(outs):
        block = value[i * capacity : (i + 1) * capacity].astype(jnp.bfloat16)
        out[0:capacity, half:] = block
        out[capacity:, half:] = block


def finish(keep, recv, far, capacity):
    rows, width = far.shape
    count = rows // capacity
    half = (width - EXTRA) // 2
    block = jax.ShapeDtypeStruct((2 * capacity, half + EXTRA), jnp.bfloat16)
    return pl.pallas_call(
        functools.partial(finish_kernel, capacity),
        out_shape=[block] * count,
        in_specs=[vmem()] * 3,
        out_specs=[vmem()] * count,
        compiler_params=params(),
        cost_estimate=cost(3 * rows * width, 10 * rows * width),
        name="finish",
    )(keep, recv, far)


def weight_kernel(group_rows, *refs):
    count = len(group_rows)
    inputs, units = refs[: 2 * count], refs[2 * count : 3 * count]
    gate_ref, up_ref, down_ref, all_units, x_rows, dy_rows = refs[3 * count :]
    hidden_units = gate_ref.shape[1]

    @pl.when(pl.program_id(0) == 0)
    def _():
        at = 0
        for rows, ref in zip(group_rows, units):
            all_units[at : at + 2 * rows, :] = ref[...]
            at += 2 * rows

    at = 0
    for g, rows in enumerate(group_rows):
        for ref in (inputs[2 * g], inputs[2 * g + 1]):
            x_rows[at : at + rows, :] = ref[0]
            dy_rows[at : at + rows, :] = ref[1]
            at += rows
    contract = (((0,), (0,)), ((), ()))
    grads = lax.dot_general(
        x_rows[...],
        all_units[:, 0 : 2 * hidden_units],
        contract,
        preferred_element_type=jnp.float32,
    )
    gate_ref[...] = grads[:, :hidden_units].astype(jnp.bfloat16)
    up_ref[...] = grads[:, hidden_units:].astype(jnp.bfloat16)
    down_ref[...] = lax.dot_general(
        all_units[:, 2 * hidden_units :],
        dy_rows[...],
        contract,
        preferred_element_type=jnp.float32,
    ).astype(jnp.bfloat16)


def weight_grads(inputs, units):
    width = inputs[0].shape[2]
    hidden_units = units[0].shape[1] // 3
    group_rows = [u.shape[0] // 2 for u in units]
    total = 2 * sum(group_rows)
    tile = 512 if width % 512 == 0 else width
    return pl.pallas_call(
        functools.partial(weight_kernel, group_rows),
        grid=(width // tile,),
        out_shape=[
            jax.ShapeDtypeStruct((width, hidden_units), jnp.bfloat16),
            jax.ShapeDtypeStruct((width, hidden_units), jnp.bfloat16),
            jax.ShapeDtypeStruct((hidden_units, width), jnp.bfloat16),
        ],
        in_specs=[pl.BlockSpec((2, a.shape[1], tile), lambda i: (0, 0, i)) for a in inputs]
        + [pl.BlockSpec(u.shape, lambda i: (0, 0)) for u in units],
        out_specs=[
            pl.BlockSpec((tile, hidden_units), lambda i: (i, 0)),
            pl.BlockSpec((tile, hidden_units), lambda i: (i, 0)),
            pl.BlockSpec((hidden_units, tile), lambda i: (0, i)),
        ],
        scratch_shapes=[
            pltpu.VMEM((total, 3 * hidden_units), jnp.bfloat16),
            pltpu.VMEM((total, tile), jnp.bfloat16),
            pltpu.VMEM((total, tile), jnp.bfloat16),
        ],
        compiler_params=params(),
        cost_estimate=cost(
            6 * total * width * hidden_units, 4 * total * width + 6 * width * hidden_units
        ),
        name="weight_grads",
    )(*inputs, *units)


def combine_kernel(expert_count, capacity, me_ref, ids_ref, weight_ref, *refs):
    blocks = refs[:expert_count]
    tok_ref, route_ref, total = refs[expert_count:]
    rows, routes = ids_ref.shape
    half = blocks[0].shape[1] - EXTRA
    lanes = 128
    me = me_ref[0]
    ids = ids_ref[...]
    lane = lax.broadcasted_iota(jnp.int32, (rows, lanes), 1)
    has = jnp.zeros((rows, lanes), jnp.float32)
    hits = [hit & (lane < expert_count) for hit in routed(me, ids, lanes)]
    for hit in hits:
        has = jnp.where(hit, 1.0, has)
    before = lax.broadcasted_iota(jnp.int32, (rows, rows), 1) < lax.broadcasted_iota(
        jnp.int32, (rows, rows), 0
    )
    rank = jnp.dot(
        before.astype(jnp.float32).astype(jnp.bfloat16),
        has.astype(jnp.bfloat16),
        preferred_element_type=jnp.float32,
    )
    slot = jnp.where(has > 0.0, rank, -1.0).astype(jnp.int32)
    index = lax.broadcasted_iota(jnp.int32, (rows, 2 * capacity), 1)
    picks = []
    for s in range(expert_count):
        column = slot[:, s : s + 1]
        low = jnp.where((column >= 0) & (column == index), 1.0, 0.0)
        high = jnp.where((column >= 0) & (column + capacity == index), 1.0, 0.0)
        low = jnp.where(index < capacity, low, 0.0)
        picks.append(jnp.concatenate([low, high], axis=0).astype(jnp.bfloat16))
    for start, size in chunks(half, 896):
        part = jnp.zeros((2 * rows, size), jnp.float32)
        for s in range(expert_count):
            part += jnp.dot(
                picks[s], blocks[s][:, start : start + size], preferred_element_type=jnp.float32
            )
        tok_ref[:, start : start + size] = part[:rows].astype(jnp.bfloat16)
        tok_ref[:, half + start : half + start + size] = part[rows:].astype(jnp.bfloat16)
    values = jnp.zeros((rows, lanes), jnp.float32)
    for s in range(expert_count):
        found = jnp.dot(picks[s], blocks[s][:, half:], preferred_element_type=jnp.float32)
        values = jnp.where(lane == s, found[:rows], values)
    total[...] = jnp.zeros_like(total)
    out = jnp.zeros((rows, lanes), jnp.float32)
    for k, hit in enumerate(hits):
        picked = jnp.sum(jnp.where(hit, values, 0.0), axis=1, keepdims=True)
        out = jnp.where(lane == k, picked, out)
    total[...] = out
    route_ref[...] = (
        total[:, 0:routes] / weight_ref[...].astype(jnp.float32)
    ).astype(jnp.bfloat16)


def combine(me, ids, weights, blocks, capacity):
    rows, routes = ids.shape
    half = blocks[0].shape[1] - EXTRA
    return pl.pallas_call(
        functools.partial(combine_kernel, len(blocks), capacity),
        out_shape=[
            jax.ShapeDtypeStruct((rows, 2 * half), jnp.bfloat16),
            jax.ShapeDtypeStruct((rows, routes), jnp.bfloat16),
        ],
        in_specs=[smem()] + [vmem()] * (2 + len(blocks)),
        out_specs=[vmem(), vmem()],
        scratch_shapes=[pltpu.VMEM((rows, 128), jnp.float32)],
        compiler_params=params(),
        cost_estimate=cost(1e9, 3e6),
        name="combine",
    )(me, ids, weights, *blocks)


def source_groups(expert_count):
    half, three = expert_count // 2, 3 * expert_count // 4
    return [
        list(range(half)),
        list(range(three, expert_count)),
        list(range(half, three)),
    ]


def shards(tokens, out_grad, expert_ids, route_weights, w_gate, w_up, w_down):
    expert_count = lax.axis_size("expert")
    group_count = lax.axis_size("dp")
    device_count = expert_count * group_count
    capacity = 5 * tokens.shape[0] // (4 * expert_count)
    if (2 * capacity) % 8:
        capacity = -(-capacity // 8) * 8
    me = lax.axis_index("expert").astype(jnp.int32).reshape(1)

    def swap(value, distance):
        return lax.ppermute(value, AXES, [(i, i ^ distance) for i in range(device_count)])

    blocks = pick_rows(
        me, expert_ids, route_weights, tokens, out_grad, expert_count, capacity
    )
    got, crossed = {}, {}
    for s in reversed(range(expert_count)):
        got[s] = swap(blocks[s], s * group_count) if s else blocks[0]
    inputs, units, back = [], [], {}
    for group in source_groups(expert_count):
        for s in group:
            crossed[s] = swap(got[s], 2)
        own = compact([got[s] for s in group] + [crossed[s] for s in group], capacity)
        other = swap(own, 1)
        keep, send, group_units = run_expert(own, other, w_gate[0], w_up[0], w_down[0])
        inputs += [own, other]
        units.append(group_units)
        recv = swap(send, 1)
        far = swap(add_half(keep, recv), 2)
        for s, block in zip(group, finish(keep, recv, far, capacity)):
            back[s] = swap(block, s * group_count) if s else block
    grad_gate, grad_up, grad_down = weight_grads(inputs, units)
    grad_tokens, grad_route = combine(
        me, expert_ids, route_weights, [back[s] for s in range(expert_count)], capacity
    )
    return (grad_tokens, grad_route, grad_gate[None], grad_up[None], grad_down[None])


def solution(mesh):
    rows = P(AXES, None)
    columns = P("expert", None, "dp")
    return jax.shard_map(
        shards,
        mesh=mesh,
        in_specs=(rows, rows, rows, rows, columns, columns, P("expert", "dp", None)),
        out_specs=(rows, rows, columns, columns, P("expert", "dp", None)),
        check_vma=False,
    )
```

```python
import functools

import jax
import jax.numpy as jnp
from jax import lax
from jax.experimental import pallas as pl
from jax.experimental.pallas import tpu as pltpu
from jax.sharding import PartitionSpec as P

AXES = ("expert", "dp")
VMEM_LIMIT = 56 * 1024 * 1024
EXTRA = 128


def vmem():
    return pl.BlockSpec(memory_space=pltpu.VMEM)


def smem():
    return pl.BlockSpec(memory_space=pltpu.SMEM)


def params():
    return pltpu.CompilerParams(vmem_limit_bytes=VMEM_LIMIT)


def cost(flops, size):
    return pl.CostEstimate(flops=int(flops), bytes_accessed=int(size), transcendentals=0)


def chunks(total, step):
    return [(start, min(step, total - start)) for start in range(0, total, step)]


def find_slots(expert_count, me, ids_t):
    rows = ids_t.shape[1]
    target = lax.broadcasted_iota(jnp.int32, (expert_count, rows), 0) ^ me
    hits = [ids_t[k : k + 1, :] == target for k in range(ids_t.shape[0])]
    has = functools.reduce(jnp.logical_or, hits)
    before = lax.broadcasted_iota(jnp.int32, (rows, rows), 0) < lax.broadcasted_iota(
        jnp.int32, (rows, rows), 1
    )
    rank = jnp.dot(
        has.astype(jnp.float32).astype(jnp.bfloat16),
        before.astype(jnp.float32).astype(jnp.bfloat16),
        preferred_element_type=jnp.float32,
    )
    return hits, jnp.where(has, rank, -1.0)


def pick_kernel(expert_count, capacity, me_ref, ids_ref, weight_ref, tok_ref, grad_ref, *refs):
    outs, pick_x, pick_dy = refs[:expert_count], refs[expert_count], refs[expert_count + 1]
    rows, width = tok_ref.shape
    hits, slot_f = find_slots(expert_count, me_ref[0], ids_ref[...])
    weights = weight_ref[...].astype(jnp.float32)
    weight = jnp.zeros((expert_count, rows), jnp.float32)
    for k, hit in enumerate(hits):
        weight = jnp.where(hit, weights[k : k + 1, :], weight)
    slot = slot_f.astype(jnp.int32)
    block = 2 * capacity
    index = lax.broadcasted_iota(jnp.int32, (block, rows), 0)
    for s in range(expert_count):
        mine = slot[s : s + 1, :]
        place = slice(s * block, (s + 1) * block)
        pick_x[place, :] = jnp.where(mine == index, 1.0, 0.0).astype(jnp.bfloat16)
        taken = (mine >= 0) & (mine + capacity == index)
        pick_dy[place, :] = jnp.where(taken, weight[s : s + 1, :], 0.0).astype(jnp.bfloat16)
    for start, size in chunks(width, 512):
        part = slice(start, start + size)
        picked = jnp.dot(pick_x[...], tok_ref[:, part], preferred_element_type=jnp.float32)
        picked += jnp.dot(pick_dy[...], grad_ref[:, part], preferred_element_type=jnp.float32)
        picked = picked.astype(jnp.bfloat16)
        for s in range(expert_count):
            outs[s][:, part] = picked[s * block : (s + 1) * block]


def pick_rows(me, ids_t, weights_t, tokens, out_grad, expert_count, capacity):
    rows, width = tokens.shape
    block = jax.ShapeDtypeStruct((2 * capacity, width), jnp.bfloat16)
    picks = pltpu.VMEM((expert_count * 2 * capacity, rows), jnp.bfloat16)
    return pl.pallas_call(
        functools.partial(pick_kernel, expert_count, capacity),
        out_shape=[block] * expert_count,
        in_specs=[smem(), vmem(), vmem(), vmem(), vmem()],
        out_specs=[vmem()] * expert_count,
        scratch_shapes=[picks, picks],
        compiler_params=params(),
        cost_estimate=cost(1e9, 4e6),
        name="pick_rows",
    )(me, ids_t, weights_t, tokens, out_grad)


NT = (((1,), (1,)), ((), ()))


def expert_kernel(tiles, capacity, count, *refs):
    blocks, weights = refs[:count], refs[count : count + 6]
    parcel_ref, keep_ref, send_ref, mine_ref = refs[count + 6 : count + 10]
    gate_w, up_w, total = refs[count + 10 :]
    gates, ups, downs = weights[0:2], weights[2:4], weights[4:6]
    step = pl.program_id(0)
    tile, units = gates[0].shape
    rows = count * capacity
    half = rows // 2
    width = tiles * tile
    x_at = pl.multiple_of(step * tile, 128)
    dy_at = pl.multiple_of(width + step * tile, 128)

    @pl.when(step == 0)
    def _():
        total[...] = jnp.zeros_like(total)

    for i, ref in enumerate(blocks):
        value = ref[...].astype(jnp.float32)
        place = slice(i * capacity, (i + 1) * capacity)
        parcel_ref[place, pl.ds(x_at, tile)] = value[:capacity].astype(jnp.bfloat16)
        parcel_ref[place, pl.ds(dy_at, tile)] = value[capacity:].astype(jnp.bfloat16)
    x = parcel_ref[:, pl.ds(x_at, tile)]
    dy = parcel_ref[:, pl.ds(dy_at, tile)]
    for core in range(2):
        gate_w[core, step] = gates[core][...]
        up_w[core, step] = ups[core][...]
        total[core, 0] += jnp.dot(x, gates[core][...], preferred_element_type=jnp.float32)
        total[core, 1] += jnp.dot(x, ups[core][...], preferred_element_type=jnp.float32)
        total[core, 2] += lax.dot_general(
            dy, downs[core][...], NT, preferred_element_type=jnp.float32
        )

    @pl.when(step == tiles - 1)
    def _():
        route = jnp.zeros((rows, 1), jnp.float32)
        unit_refs = (mine_ref, parcel_ref.at[:, 2 * width :])
        for core, out in enumerate(unit_refs):
            gate_value = total[core, 0]
            up_value = total[core, 1]
            back = total[core, 2]
            sigmoid = jax.nn.sigmoid(gate_value)
            silu = gate_value * sigmoid
            hidden = (silu * up_value).astype(jnp.bfloat16)
            d_gate = back * up_value * sigmoid * (1.0 + gate_value * (1.0 - sigmoid))
            out[:, 0:units] = d_gate.astype(jnp.bfloat16)
            out[:, units : 2 * units] = (back * silu).astype(jnp.bfloat16)
            out[:, 2 * units :] = hidden
            route += jnp.sum(hidden.astype(jnp.float32) * back, axis=1, keepdims=True)
        route = jnp.broadcast_to(route, (rows, EXTRA)).astype(jnp.bfloat16)
        keep_ref[:, width:] = route[:half]
        send_ref[:, width:] = route[half:]
        for at in range(tiles):
            part = jnp.zeros((rows, tile), jnp.float32)
            for core, out in enumerate(unit_refs):
                part += lax.dot_general(
                    out[:, 0:units], gate_w[core, at], NT, preferred_element_type=jnp.float32
                )
                part += lax.dot_general(
                    out[:, units : 2 * units],
                    up_w[core, at],
                    NT,
                    preferred_element_type=jnp.float32,
                )
            part = part.astype(jnp.bfloat16)
            keep_ref[:, at * tile : (at + 1) * tile] = part[:half]
            send_ref[:, at * tile : (at + 1) * tile] = part[half:]


def run_expert(blocks, weights, capacity):
    width = blocks[0].shape[1]
    units = weights[0].shape[1]
    count = len(blocks)
    rows = count * capacity
    tile = width // 4 if width % 512 == 0 else width
    tiles = width // tile
    out = jax.ShapeDtypeStruct((rows // 2, width + EXTRA), jnp.bfloat16)
    unit_rows = jax.ShapeDtypeStruct((rows, 3 * units), jnp.bfloat16)
    parcel = jax.ShapeDtypeStruct((rows, 2 * width + 3 * units), jnp.bfloat16)

    def whole(shape):
        return pl.BlockSpec(shape, lambda i: (0, 0))

    return pl.pallas_call(
        functools.partial(expert_kernel, tiles, capacity, count),
        grid=(tiles,),
        out_shape=[parcel, out, out, unit_rows],
        in_specs=[pl.BlockSpec((2 * capacity, tile), lambda i: (0, i))] * count
        + [pl.BlockSpec((tile, units), lambda i: (i, 0))] * 4
        + [pl.BlockSpec((units, tile), lambda i: (0, i))] * 2,
        out_specs=[
            whole(parcel.shape),
            whole(out.shape),
            whole(out.shape),
            whole(unit_rows.shape),
        ],
        scratch_shapes=[
            pltpu.VMEM((2, tiles, tile, units), jnp.bfloat16),
            pltpu.VMEM((2, tiles, tile, units), jnp.bfloat16),
            pltpu.VMEM((2, 3, rows, units), jnp.float32),
        ],
        compiler_params=params(),
        cost_estimate=cost(20 * rows * width * units, 12 * width * units + 10 * rows * width),
        name="run_expert",
    )(*blocks, *weights)


def finish_kernel(capacity, keep_ref, far_ref, *outs):
    half = (far_ref.shape[1] - EXTRA) // 2

    def summed(part):
        return keep_ref[:, part].astype(jnp.float32) + far_ref[:, part].astype(jnp.float32)

    for h in range(2):
        for start, size in chunks(half, 896):
            value = summed(slice(h * half + start, h * half + start + size))
            for i, out in enumerate(outs):
                out[h * capacity : (h + 1) * capacity, start : start + size] = value[
                    i * capacity : (i + 1) * capacity
                ].astype(jnp.bfloat16)
    value = summed(slice(2 * half, 2 * half + EXTRA))
    for i, out in enumerate(outs):
        block = value[i * capacity : (i + 1) * capacity].astype(jnp.bfloat16)
        out[0:capacity, half:] = block
        out[capacity:, half:] = block


def finish(keep, far, capacity):
    rows, width = far.shape
    count = rows // capacity
    half = (width - EXTRA) // 2
    block = jax.ShapeDtypeStruct((2 * capacity, half + EXTRA), jnp.bfloat16)
    return pl.pallas_call(
        functools.partial(finish_kernel, capacity),
        out_shape=[block] * count,
        in_specs=[vmem()] * 2,
        out_specs=[vmem()] * count,
        compiler_params=params(),
        cost_estimate=cost(2 * rows * width, 6 * rows * width),
        name="finish",
    )(keep, far)


def weight_kernel(group_rows, *refs):
    count = len(group_rows)
    x_refs, dy_refs = refs[:count], refs[count : 2 * count]
    unit_refs = refs[2 * count : 5 * count]
    gate_ref, up_ref, down_ref, all_units, x_rows, dy_rows = refs[5 * count :]
    units = gate_ref.shape[1]

    @pl.when(pl.program_id(0) == 0)
    def _():
        at = 0
        for g, rows in enumerate(group_rows):
            for part in range(3):
                all_units[at : at + rows, part * units : (part + 1) * units] = unit_refs[
                    3 * g + part
                ][...]
            at += rows

    at = 0
    for rows, x_ref, dy_ref in zip(group_rows, x_refs, dy_refs):
        x_rows[at : at + rows, :] = x_ref[...]
        dy_rows[at : at + rows, :] = dy_ref[...]
        at += rows
    contract = (((0,), (0,)), ((), ()))
    grads = lax.dot_general(
        x_rows[...], all_units[:, 0 : 2 * units], contract, preferred_element_type=jnp.float32
    )
    gate_ref[...] = grads[:, :units].astype(jnp.bfloat16)
    up_ref[...] = grads[:, units:].astype(jnp.bfloat16)
    down_ref[...] = lax.dot_general(
        all_units[:, 2 * units :], dy_rows[...], contract, preferred_element_type=jnp.float32
    ).astype(jnp.bfloat16)


def weight_grads(parcels, units, width):
    hidden_units = (parcels[0].shape[1] - 2 * width) // 3
    group_rows = [p.shape[0] for p in parcels]
    total = sum(group_rows)
    tile = 512 if width % 512 == 0 else width
    tiles = width // tile
    unit_at = 2 * width // hidden_units
    unit_args, unit_specs = [], []
    for parcel, own in zip(parcels, units):
        shape = (parcel.shape[0], hidden_units)
        first = unit_at if own is None else 0
        for part in range(3):
            unit_args.append(parcel if own is None else own)
            unit_specs.append(pl.BlockSpec(shape, lambda i, at=first + part: (0, at)))
    return pl.pallas_call(
        functools.partial(weight_kernel, group_rows),
        grid=(tiles,),
        out_shape=[
            jax.ShapeDtypeStruct((width, hidden_units), jnp.bfloat16),
            jax.ShapeDtypeStruct((width, hidden_units), jnp.bfloat16),
            jax.ShapeDtypeStruct((hidden_units, width), jnp.bfloat16),
        ],
        in_specs=[pl.BlockSpec((rows, tile), lambda i: (0, i)) for rows in group_rows]
        + [pl.BlockSpec((rows, tile), lambda i: (0, tiles + i)) for rows in group_rows]
        + unit_specs,
        out_specs=[
            pl.BlockSpec((tile, hidden_units), lambda i: (i, 0)),
            pl.BlockSpec((tile, hidden_units), lambda i: (i, 0)),
            pl.BlockSpec((hidden_units, tile), lambda i: (0, i)),
        ],
        scratch_shapes=[
            pltpu.VMEM((total, 3 * hidden_units), jnp.bfloat16),
            pltpu.VMEM((total, tile), jnp.bfloat16),
            pltpu.VMEM((total, tile), jnp.bfloat16),
        ],
        compiler_params=params(),
        cost_estimate=cost(
            6 * total * width * hidden_units, 4 * total * width + 6 * width * hidden_units
        ),
        name="weight_grads",
    )(*parcels, *parcels, *unit_args)


def combine_kernel(expert_count, capacity, me_ref, ids_ref, weight_ref, *refs):
    blocks = refs[:expert_count]
    tok_ref, route_ref, slots, values = refs[expert_count:]
    routes, rows = ids_ref.shape
    half = blocks[0].shape[1] - EXTRA
    hits, slot_t = find_slots(expert_count, me_ref[0], ids_ref[...])
    slots[...] = jnp.full(slots.shape, -1.0, jnp.float32)
    slots[0:expert_count, :] = slot_t
    slot = slots[...].T.astype(jnp.int32)
    lane = lax.broadcasted_iota(jnp.int32, (rows, slots.shape[0]), 1)
    index = lax.broadcasted_iota(jnp.int32, (rows, 2 * capacity), 1)
    picks = []
    for s in range(expert_count):
        column = slot[:, s : s + 1]
        low = jnp.where(column == index, 1.0, 0.0)
        high = jnp.where((column >= 0) & (column + capacity == index), 1.0, 0.0)
        picks.append(jnp.concatenate([low, high], axis=0).astype(jnp.bfloat16))
    for start, size in chunks(half, 896):
        part = jnp.zeros((2 * rows, size), jnp.float32)
        for s in range(expert_count):
            part += jnp.dot(
                picks[s], blocks[s][:, start : start + size], preferred_element_type=jnp.float32
            )
        tok_ref[:, start : start + size] = part[:rows].astype(jnp.bfloat16)
        tok_ref[:, half + start : half + start + size] = part[rows:].astype(jnp.bfloat16)
    value = jnp.zeros((rows, slots.shape[0]), jnp.float32)
    for s in range(expert_count):
        found = jnp.dot(picks[s], blocks[s][:, half:], preferred_element_type=jnp.float32)
        value = jnp.where(lane == s, found[:rows, 0:1], value)
    values[...] = value.T
    value_t = values[0:expert_count, :]
    weights = weight_ref[...].astype(jnp.float32)
    found = [
        jnp.sum(jnp.where(hit, value_t, 0.0), axis=0, keepdims=True) for hit in hits
    ]
    route_ref[...] = (jnp.concatenate(found, axis=0) / weights).astype(jnp.bfloat16)


def combine(me, ids_t, weights_t, blocks, capacity):
    routes, rows = ids_t.shape
    half = blocks[0].shape[1] - EXTRA
    return pl.pallas_call(
        functools.partial(combine_kernel, len(blocks), capacity),
        out_shape=[
            jax.ShapeDtypeStruct((rows, 2 * half), jnp.bfloat16),
            jax.ShapeDtypeStruct((routes, rows), jnp.bfloat16),
        ],
        in_specs=[smem()] + [vmem()] * (2 + len(blocks)),
        out_specs=[vmem(), vmem()],
        scratch_shapes=[pltpu.VMEM((128, rows), jnp.float32), pltpu.VMEM((128, rows), jnp.float32)],
        compiler_params=params(),
        cost_estimate=cost(1e9, 3e6),
        name="combine",
    )(me, ids_t, weights_t, *blocks)


def source_groups(expert_count):
    half, three = expert_count // 2, 3 * expert_count // 4
    return [
        list(range(half)),
        list(range(three, expert_count)),
        list(range(half, three)),
    ]


def after(*values):
    return lax.optimization_barrier(values)


def shards(tokens, out_grad, expert_ids, route_weights, w_gate, w_up, w_down):
    expert_count = lax.axis_size("expert")
    group_count = lax.axis_size("dp")
    device_count = expert_count * group_count
    capacity = 5 * tokens.shape[0] // (4 * expert_count)
    if (2 * capacity) % 8:
        capacity = -(-capacity // 8) * 8
    me = lax.axis_index("expert").astype(jnp.int32).reshape(1)
    ids_t, weights_t = expert_ids.T, route_weights.T

    def swap(value, distance):
        return lax.ppermute(value, AXES, [(i, i ^ distance) for i in range(device_count)])

    near, first, second = source_groups(expert_count)
    got, crossed, back = {}, {}, {}
    parcels, units = [], []

    def fetch(group, source):
        for s in group:
            got[s] = swap(source[s], s * group_count) if s else source[s]

    def cross(group):
        for s in group:
            crossed[s] = swap(got[s], 2)

    def work(group):
        parcel, keep, send, mine = run_expert(
            [got[s] for s in group] + [crossed[s] for s in group], weights, capacity
        )
        parcels.append(parcel)
        units.append(mine)
        return parcel, keep, send

    def ready(group, keep, far):
        return dict(zip(group, finish(keep, far, capacity)))

    def give(blocks):
        for s, block in blocks.items():
            back[s] = swap(block, s * group_count) if s else block

    weights = []
    for own in (w_gate[0], w_up[0], w_down[0]):
        weights += [own, swap(own, 1)]
    blocks = list(pick_rows(me, ids_t, weights_t, tokens, out_grad, expert_count, capacity))
    fetch(first, blocks)
    weights, close = after(weights, {s: blocks[s] for s in near})
    fetch(near, close)
    cross(near[:2])
    got, crossed, later = after(got, crossed, {s: blocks[s] for s in second})
    fetch(second, later)
    cross(near[2:])
    cross(first)
    near_parcel, near_keep, near_send = work(near)
    near_far = swap(near_send, 2)
    first_parcel, first_keep, first_send = work(first)
    first_far = swap(first_send, 2)
    moved = {s: got[s] for s in second}
    near_keep, first_keep, moved = after(near_keep, first_keep, moved)
    got.update(moved)
    cross(second)
    near_ready = ready(near, near_keep, near_far)
    first_ready = ready(first, first_keep, first_far)
    moved = {s: crossed[s] for s in second}
    near_ready, first_ready, moved = after(near_ready, first_ready, moved)
    crossed.update(moved)
    give(first_ready)
    give(near_ready)
    second_parcel, second_keep, second_send = work(second)
    back, second_send, parcels = after(back, second_send, parcels)
    second_far = swap(second_send, 2)
    others = [swap(parcel, 1) for parcel in parcels]
    second_ready = ready(second, second_keep, second_far)
    others, second_ready = after(others, second_ready)
    give(second_ready)
    grads = weight_grads(parcels + others, units + [None] * 3, tokens.shape[1])
    grads, back = after(list(grads), back)
    grad_gate, grad_up, grad_down = grads
    grad_tokens, grad_route_t = combine(
        me, ids_t, weights_t, [back[s] for s in range(expert_count)], capacity
    )
    return (grad_tokens, grad_route_t.T, grad_gate[None], grad_up[None], grad_down[None])


def solution(mesh):
    rows = P(AXES, None)
    columns = P("expert", None, "dp")
    return jax.shard_map(
        shards,
        mesh=mesh,
        in_specs=(rows, rows, rows, rows, columns, columns, P("expert", "dp", None)),
        out_specs=(rows, rows, columns, columns, P("expert", "dp", None)),
        check_vma=False,
    )
```

```python
import functools

import jax
import jax.numpy as jnp
from jax import lax
from jax.experimental import pallas as pl
from jax.experimental.pallas import tpu as pltpu
from jax.sharding import PartitionSpec as P

AXES = ("expert", "dp")
VMEM_LIMIT = 24 * 1024 * 1024
EXTRA = 128
EXPERT_VMEM = 24 * 1024 * 1024


def vmem():
    return pl.BlockSpec(memory_space=pltpu.VMEM)


def smem():
    return pl.BlockSpec(memory_space=pltpu.SMEM)


def params():
    return pltpu.CompilerParams(vmem_limit_bytes=VMEM_LIMIT)


def cost(flops, size):
    return pl.CostEstimate(flops=int(flops), bytes_accessed=int(size), transcendentals=0)


def chunks(total, step):
    return [(start, min(step, total - start)) for start in range(0, total, step)]


def find_slots(expert_count, me, ids_t):
    rows = ids_t.shape[1]
    target = lax.broadcasted_iota(jnp.int32, (expert_count, rows), 0) ^ me
    hits = [ids_t[k : k + 1, :] == target for k in range(ids_t.shape[0])]
    has = functools.reduce(jnp.logical_or, hits)
    before = lax.broadcasted_iota(jnp.int32, (rows, rows), 0) < lax.broadcasted_iota(
        jnp.int32, (rows, rows), 1
    )
    rank = jnp.dot(
        has.astype(jnp.float32).astype(jnp.bfloat16),
        before.astype(jnp.float32).astype(jnp.bfloat16),
        preferred_element_type=jnp.float32,
    )
    return hits, jnp.where(has, rank, -1.0)


def pick_kernel(expert_count, capacity, me_ref, ids_ref, weight_ref, tok_ref, grad_ref, *refs):
    outs, pick_x, pick_dy = refs[:expert_count], refs[expert_count], refs[expert_count + 1]
    rows, width = tok_ref.shape
    hits, slot_f = find_slots(expert_count, me_ref[0], ids_ref[...])
    weights = weight_ref[...].astype(jnp.float32)
    weight = jnp.zeros((expert_count, rows), jnp.float32)
    for k, hit in enumerate(hits):
        weight = jnp.where(hit, weights[k : k + 1, :], weight)
    slot = slot_f.astype(jnp.int32)
    block = 2 * capacity
    index = lax.broadcasted_iota(jnp.int32, (block, rows), 0)
    for s in range(expert_count):
        mine = slot[s : s + 1, :]
        place = slice(s * block, (s + 1) * block)
        pick_x[place, :] = jnp.where(mine == index, 1.0, 0.0).astype(jnp.bfloat16)
        taken = (mine >= 0) & (mine + capacity == index)
        pick_dy[place, :] = jnp.where(taken, weight[s : s + 1, :], 0.0).astype(jnp.bfloat16)
    for start, size in chunks(width, 512):
        part = slice(start, start + size)
        picked = jnp.dot(pick_x[...], tok_ref[:, part], preferred_element_type=jnp.float32)
        picked += jnp.dot(pick_dy[...], grad_ref[:, part], preferred_element_type=jnp.float32)
        picked = picked.astype(jnp.bfloat16)
        for s in range(expert_count):
            outs[s][:, part] = picked[s * block : (s + 1) * block]


def pick_rows(me, ids_t, weights_t, tokens, out_grad, expert_count, capacity):
    rows, width = tokens.shape
    block = jax.ShapeDtypeStruct((2 * capacity, width), jnp.bfloat16)
    picks = pltpu.VMEM((expert_count * 2 * capacity, rows), jnp.bfloat16)
    return pl.pallas_call(
        functools.partial(pick_kernel, expert_count, capacity),
        out_shape=[block] * expert_count,
        in_specs=[smem(), vmem(), vmem(), vmem(), vmem()],
        out_specs=[vmem()] * expert_count,
        scratch_shapes=[picks, picks],
        compiler_params=params(),
        cost_estimate=cost(1e9, 4e6),
        name="pick_rows",
    )(me, ids_t, weights_t, tokens, out_grad)


NT = (((1,), (1,)), ((), ()))


def expert_kernel(capacity, count, groups, *refs):
    blocks, weights = refs[:count], refs[count : count + 6]
    parcel_ref, mine_ref = refs[count + 6 : count + 8]
    keep_refs = refs[count + 8 : count + 8 + len(groups)]
    send_refs = refs[count + 8 + len(groups) :]
    gates, ups, downs = weights[0:2], weights[2:4], weights[4:6]
    width, units = gates[0].shape
    rows = count * capacity
    tiles = chunks(width, 896)
    totals = [[jnp.zeros((rows, units), jnp.float32)] * 3 for _ in range(2)]
    for at, tile in tiles:
        here = slice(at, at + tile)
        there = slice(width + at, width + at + tile)
        for i, ref in enumerate(blocks):
            value = ref[:, here].astype(jnp.float32)
            place = slice(i * capacity, (i + 1) * capacity)
            parcel_ref[place, here] = value[:capacity].astype(jnp.bfloat16)
            parcel_ref[place, there] = value[capacity:].astype(jnp.bfloat16)
        x = parcel_ref[:, here]
        dy = parcel_ref[:, there]
        for core, total in enumerate(totals):
            total[0] += jnp.dot(x, gates[core][here, :], preferred_element_type=jnp.float32)
            total[1] += jnp.dot(x, ups[core][here, :], preferred_element_type=jnp.float32)
            total[2] += lax.dot_general(
                dy, downs[core][:, here], NT, preferred_element_type=jnp.float32
            )
    route = jnp.zeros((rows, 1), jnp.float32)
    unit_refs = (mine_ref, parcel_ref.at[:, 2 * width :])
    for (gate_value, up_value, back), out in zip(totals, unit_refs):
        sigmoid = jax.nn.sigmoid(gate_value)
        silu = gate_value * sigmoid
        hidden = (silu * up_value).astype(jnp.bfloat16)
        d_gate = back * up_value * sigmoid * (1.0 + gate_value * (1.0 - sigmoid))
        out[:, 0:units] = d_gate.astype(jnp.bfloat16)
        out[:, units : 2 * units] = (back * silu).astype(jnp.bfloat16)
        out[:, 2 * units :] = hidden
        route += jnp.sum(hidden.astype(jnp.float32) * back, axis=1, keepdims=True)

    def put(value, here):
        value = value.astype(jnp.bfloat16)
        for out_refs, at in ((keep_refs, 0), (send_refs, rows // 2)):
            for out, size in zip(out_refs, groups):
                out[:, here] = value[at : at + size * capacity]
                at += size * capacity

    put(jnp.broadcast_to(route, (rows, EXTRA)), slice(width, width + EXTRA))
    for at, tile in tiles:
        here = slice(at, at + tile)
        part = jnp.zeros((rows, tile), jnp.float32)
        for core, out in enumerate(unit_refs):
            part += lax.dot_general(
                out[:, 0:units], gates[core][here, :], NT, preferred_element_type=jnp.float32
            )
            part += lax.dot_general(
                out[:, units : 2 * units],
                ups[core][here, :],
                NT,
                preferred_element_type=jnp.float32,
            )
        put(part, here)


def run_expert(blocks, weights, capacity, groups):
    width = blocks[0].shape[1]
    units = weights[0].shape[1]
    count = len(blocks)
    rows = count * capacity
    outs = [jax.ShapeDtypeStruct((size * capacity, width + EXTRA), jnp.bfloat16) for size in groups]
    unit_rows = jax.ShapeDtypeStruct((rows, 3 * units), jnp.bfloat16)
    parcel = jax.ShapeDtypeStruct((rows, 2 * width + 3 * units), jnp.bfloat16)
    out = pl.pallas_call(
        functools.partial(expert_kernel, capacity, count, groups),
        out_shape=[parcel, unit_rows] + outs + outs,
        in_specs=[vmem()] * (count + 6),
        out_specs=[vmem()] * (2 + 2 * len(groups)),
        compiler_params=pltpu.CompilerParams(vmem_limit_bytes=EXPERT_VMEM),
        cost_estimate=cost(20 * rows * width * units, 12 * width * units + 10 * rows * width),
        name="run_expert",
    )(*blocks, *weights)
    return out[0], out[1], out[2 : 2 + len(groups)], out[2 + len(groups) :]


def finish_kernel(capacity, keep_ref, far_ref, *outs):
    half = (far_ref.shape[1] - EXTRA) // 2

    def summed(part):
        return keep_ref[:, part].astype(jnp.float32) + far_ref[:, part].astype(jnp.float32)

    for h in range(2):
        for start, size in chunks(half, 896):
            value = summed(slice(h * half + start, h * half + start + size))
            for i, out in enumerate(outs):
                out[h * capacity : (h + 1) * capacity, start : start + size] = value[
                    i * capacity : (i + 1) * capacity
                ].astype(jnp.bfloat16)
    value = summed(slice(2 * half, 2 * half + EXTRA))
    for i, out in enumerate(outs):
        block = value[i * capacity : (i + 1) * capacity].astype(jnp.bfloat16)
        out[0:capacity, half:] = block
        out[capacity:, half:] = block


def finish(keep, far, capacity):
    rows, width = far.shape
    count = rows // capacity
    half = (width - EXTRA) // 2
    block = jax.ShapeDtypeStruct((2 * capacity, half + EXTRA), jnp.bfloat16)
    return pl.pallas_call(
        functools.partial(finish_kernel, capacity),
        out_shape=[block] * count,
        in_specs=[vmem()] * 2,
        out_specs=[vmem()] * count,
        compiler_params=params(),
        cost_estimate=cost(2 * rows * width, 6 * rows * width),
        name="finish",
    )(keep, far)


def weight_kernel(group_rows, *refs):
    count = len(group_rows)
    x_refs, dy_refs = refs[:count], refs[count : 2 * count]
    unit_refs = refs[2 * count : 5 * count]
    gate_ref, up_ref, down_ref, all_units, x_rows, dy_rows = refs[5 * count :]
    units = gate_ref.shape[1]

    @pl.when(pl.program_id(0) == 0)
    def _():
        at = 0
        for g, rows in enumerate(group_rows):
            for part in range(3):
                all_units[at : at + rows, part * units : (part + 1) * units] = unit_refs[
                    3 * g + part
                ][...]
            at += rows

    at = 0
    for rows, x_ref, dy_ref in zip(group_rows, x_refs, dy_refs):
        x_rows[at : at + rows, :] = x_ref[...]
        dy_rows[at : at + rows, :] = dy_ref[...]
        at += rows
    contract = (((0,), (0,)), ((), ()))
    grads = lax.dot_general(
        x_rows[...], all_units[:, 0 : 2 * units], contract, preferred_element_type=jnp.float32
    )
    gate_ref[...] = grads[:, :units].astype(jnp.bfloat16)
    up_ref[...] = grads[:, units:].astype(jnp.bfloat16)
    down_ref[...] = lax.dot_general(
        all_units[:, 2 * units :], dy_rows[...], contract, preferred_element_type=jnp.float32
    ).astype(jnp.bfloat16)


def weight_grads(parcels, units, width):
    hidden_units = (parcels[0].shape[1] - 2 * width) // 3
    group_rows = [p.shape[0] for p in parcels]
    total = sum(group_rows)
    tile = 512 if width % 512 == 0 else width
    tiles = width // tile
    unit_at = 2 * width // hidden_units
    unit_args, unit_specs = [], []
    for parcel, own in zip(parcels, units):
        shape = (parcel.shape[0], hidden_units)
        first = unit_at if own is None else 0
        for part in range(3):
            unit_args.append(parcel if own is None else own)
            unit_specs.append(pl.BlockSpec(shape, lambda i, at=first + part: (0, at)))
    return pl.pallas_call(
        functools.partial(weight_kernel, group_rows),
        grid=(tiles,),
        out_shape=[
            jax.ShapeDtypeStruct((width, hidden_units), jnp.bfloat16),
            jax.ShapeDtypeStruct((width, hidden_units), jnp.bfloat16),
            jax.ShapeDtypeStruct((hidden_units, width), jnp.bfloat16),
        ],
        in_specs=[pl.BlockSpec((rows, tile), lambda i: (0, i)) for rows in group_rows]
        + [pl.BlockSpec((rows, tile), lambda i: (0, tiles + i)) for rows in group_rows]
        + unit_specs,
        out_specs=[
            pl.BlockSpec((tile, hidden_units), lambda i: (i, 0)),
            pl.BlockSpec((tile, hidden_units), lambda i: (i, 0)),
            pl.BlockSpec((hidden_units, tile), lambda i: (0, i)),
        ],
        scratch_shapes=[
            pltpu.VMEM((total, 3 * hidden_units), jnp.bfloat16),
            pltpu.VMEM((total, tile), jnp.bfloat16),
            pltpu.VMEM((total, tile), jnp.bfloat16),
        ],
        compiler_params=params(),
        cost_estimate=cost(
            6 * total * width * hidden_units, 4 * total * width + 6 * width * hidden_units
        ),
        name="weight_grads",
    )(*parcels, *parcels, *unit_args)


def combine_kernel(expert_count, capacity, me_ref, ids_ref, weight_ref, *refs):
    blocks = refs[:expert_count]
    tok_ref, route_ref, slots, values = refs[expert_count:]
    routes, rows = ids_ref.shape
    half = blocks[0].shape[1] - EXTRA
    hits, slot_t = find_slots(expert_count, me_ref[0], ids_ref[...])
    slots[...] = jnp.full(slots.shape, -1.0, jnp.float32)
    slots[0:expert_count, :] = slot_t
    slot = slots[...].T.astype(jnp.int32)
    lane = lax.broadcasted_iota(jnp.int32, (rows, slots.shape[0]), 1)
    index = lax.broadcasted_iota(jnp.int32, (rows, 2 * capacity), 1)
    picks = []
    for s in range(expert_count):
        column = slot[:, s : s + 1]
        low = jnp.where(column == index, 1.0, 0.0)
        high = jnp.where((column >= 0) & (column + capacity == index), 1.0, 0.0)
        picks.append(jnp.concatenate([low, high], axis=0).astype(jnp.bfloat16))
    for start, size in chunks(half, 896):
        part = jnp.zeros((2 * rows, size), jnp.float32)
        for s in range(expert_count):
            part += jnp.dot(
                picks[s], blocks[s][:, start : start + size], preferred_element_type=jnp.float32
            )
        tok_ref[:, start : start + size] = part[:rows].astype(jnp.bfloat16)
        tok_ref[:, half + start : half + start + size] = part[rows:].astype(jnp.bfloat16)
    value = jnp.zeros((rows, slots.shape[0]), jnp.float32)
    for s in range(expert_count):
        found = jnp.dot(picks[s], blocks[s][:, half:], preferred_element_type=jnp.float32)
        value = jnp.where(lane == s, found[:rows, 0:1], value)
    values[...] = value.T
    value_t = values[0:expert_count, :]
    weights = weight_ref[...].astype(jnp.float32)
    found = [
        jnp.sum(jnp.where(hit, value_t, 0.0), axis=0, keepdims=True) for hit in hits
    ]
    route_ref[...] = (jnp.concatenate(found, axis=0) / weights).astype(jnp.bfloat16)


def combine(me, ids_t, weights_t, blocks, capacity):
    routes, rows = ids_t.shape
    half = blocks[0].shape[1] - EXTRA
    return pl.pallas_call(
        functools.partial(combine_kernel, len(blocks), capacity),
        out_shape=[
            jax.ShapeDtypeStruct((rows, 2 * half), jnp.bfloat16),
            jax.ShapeDtypeStruct((routes, rows), jnp.bfloat16),
        ],
        in_specs=[smem()] + [vmem()] * (2 + len(blocks)),
        out_specs=[vmem(), vmem()],
        scratch_shapes=[pltpu.VMEM((128, rows), jnp.float32), pltpu.VMEM((128, rows), jnp.float32)],
        compiler_params=params(),
        cost_estimate=cost(1e9, 3e6),
        name="combine",
    )(me, ids_t, weights_t, *blocks)


def source_groups(expert_count):
    half, three = expert_count // 2, 3 * expert_count // 4
    return [
        list(range(half)),
        list(range(three, expert_count)),
        list(range(half, three)),
    ]


def after(*values):
    return lax.optimization_barrier(values)


def shards(tokens, out_grad, expert_ids, route_weights, w_gate, w_up, w_down):
    expert_count = lax.axis_size("expert")
    group_count = lax.axis_size("dp")
    device_count = expert_count * group_count
    capacity = 5 * tokens.shape[0] // (4 * expert_count)
    if (2 * capacity) % 8:
        capacity = -(-capacity // 8) * 8
    me = lax.axis_index("expert").astype(jnp.int32).reshape(1)
    ids_t, weights_t = expert_ids.T, route_weights.T

    def swap(value, distance):
        return lax.ppermute(value, AXES, [(i, i ^ distance) for i in range(device_count)])

    near, first, second = source_groups(expert_count)
    got, crossed, back = {}, {}, {}

    def fetch(group, source):
        for s in group:
            got[s] = swap(source[s], s * group_count) if s else source[s]

    def cross(group):
        for s in group:
            crossed[s] = swap(got[s], 2)

    def ready(group, keep, far):
        return dict(zip(group, finish(keep, far, capacity)))

    def give(blocks):
        for s, block in blocks.items():
            back[s] = swap(block, s * group_count) if s else block

    weights = []
    for own in (w_gate[0], w_up[0], w_down[0]):
        weights += [own, swap(own, 1)]
    blocks = list(pick_rows(me, ids_t, weights_t, tokens, out_grad, expert_count, capacity))
    fetch(first, blocks)
    weights, close = after(weights, {s: blocks[s] for s in near})
    fetch(near, close)
    cross(near[:-1])
    early, waiting = {s: crossed[s] for s in near[:-2]}, {s: blocks[s] for s in second}
    got, early, weights, waiting = after(got, early, weights, waiting)
    crossed.update(early)
    fetch(second, waiting)
    cross(near[-1:] + first)
    got, crossed = after(got, crossed)
    cross(second)

    def work(*groups):
        order = sum(groups, [])
        return run_expert(
            [got[s] for s in order] + [crossed[s] for s in order],
            weights,
            capacity,
            [len(group) for group in groups],
        )

    parcel, units, keeps, sends = work(first, near)
    ahead = {s: crossed[s] for s in second}
    keeps, ahead = after(keeps, ahead)
    crossed.update(ahead)
    last_parcel, last_units, last_keeps, last_sends = work(second)
    first_far = swap(sends[0], 2)
    first_ready = ready(first, keeps[0], first_far)
    first_ready, last_sends, parcel = after(first_ready, last_sends, parcel)
    give(first_ready)
    second_far = swap(last_sends[0], 2)
    near_far = swap(sends[1], 2)
    second_ready = ready(second, last_keeps[0], second_far)
    other = swap(parcel, 1)
    returned = {s: back[s] for s in first}
    returned, near_far, second_ready, other, last_parcel = after(
        returned, near_far, second_ready, other, last_parcel
    )
    back.update(returned)
    give(second_ready)
    last_other = swap(last_parcel, 1)
    near_ready = ready(near, keeps[1], near_far)
    last_other, near_ready = after(last_other, near_ready)
    give(near_ready)
    parcels = [parcel, last_parcel, other, last_other]
    grads = weight_grads(parcels, [units, last_units, None, None], tokens.shape[1])
    grads, back = after(list(grads), back)
    grad_gate, grad_up, grad_down = grads
    grad_tokens, grad_route_t = combine(
        me, ids_t, weights_t, [back[s] for s in range(expert_count)], capacity
    )
    return (grad_tokens, grad_route_t.T, grad_gate[None], grad_up[None], grad_down[None])


def solution(mesh):
    rows = P(AXES, None)
    columns = P("expert", None, "dp")
    return jax.shard_map(
        shards,
        mesh=mesh,
        in_specs=(rows, rows, rows, rows, columns, columns, P("expert", "dp", None)),
        out_specs=(rows, rows, columns, columns, P("expert", "dp", None)),
        check_vma=False,
    )
```

```python
import functools

import jax
import jax.numpy as jnp
from jax import lax
from jax.experimental import pallas as pl
from jax.experimental.pallas import tpu as pltpu
from jax.sharding import PartitionSpec as P

AXES = ("expert", "dp")
VMEM_LIMIT = 24 * 1024 * 1024
EXTRA = 128
EXPERT_VMEM = 24 * 1024 * 1024


def vmem():
    return pl.BlockSpec(memory_space=pltpu.VMEM)


def smem():
    return pl.BlockSpec(memory_space=pltpu.SMEM)


def params():
    return pltpu.CompilerParams(vmem_limit_bytes=VMEM_LIMIT)


def cost(flops, size):
    return pl.CostEstimate(flops=int(flops), bytes_accessed=int(size), transcendentals=0)


def chunks(total, step):
    return [(start, min(step, total - start)) for start in range(0, total, step)]


def find_slots(expert_count, me, ids_t):
    rows = ids_t.shape[1]
    target = lax.broadcasted_iota(jnp.int32, (expert_count, rows), 0) ^ me
    hits = [ids_t[k : k + 1, :] == target for k in range(ids_t.shape[0])]
    has = functools.reduce(jnp.logical_or, hits)
    before = lax.broadcasted_iota(jnp.int32, (rows, rows), 0) < lax.broadcasted_iota(
        jnp.int32, (rows, rows), 1
    )
    rank = jnp.dot(
        has.astype(jnp.float32).astype(jnp.bfloat16),
        before.astype(jnp.float32).astype(jnp.bfloat16),
        preferred_element_type=jnp.float32,
    )
    return hits, jnp.where(has, rank, -1.0)


def pick_kernel(expert_count, capacity, me_ref, ids_ref, weight_ref, tok_ref, grad_ref, *refs):
    outs, pick_x, pick_dy = refs[:expert_count], refs[expert_count], refs[expert_count + 1]
    rows, width = tok_ref.shape
    hits, slot_f = find_slots(expert_count, me_ref[0], ids_ref[...])
    weights = weight_ref[...].astype(jnp.float32)
    weight = jnp.zeros((expert_count, rows), jnp.float32)
    for k, hit in enumerate(hits):
        weight = jnp.where(hit, weights[k : k + 1, :], weight)
    slot = slot_f.astype(jnp.int32)
    block = 2 * capacity
    index = lax.broadcasted_iota(jnp.int32, (block, rows), 0)
    for s in range(expert_count):
        mine = slot[s : s + 1, :]
        place = slice(s * block, (s + 1) * block)
        pick_x[place, :] = jnp.where(mine == index, 1.0, 0.0).astype(jnp.bfloat16)
        taken = (mine >= 0) & (mine + capacity == index)
        pick_dy[place, :] = jnp.where(taken, weight[s : s + 1, :], 0.0).astype(jnp.bfloat16)
    for start, size in chunks(width, 512):
        part = slice(start, start + size)
        picked = jnp.dot(pick_x[...], tok_ref[:, part], preferred_element_type=jnp.float32)
        picked += jnp.dot(pick_dy[...], grad_ref[:, part], preferred_element_type=jnp.float32)
        picked = picked.astype(jnp.bfloat16)
        for s in range(expert_count):
            outs[s][:, part] = picked[s * block : (s + 1) * block]


def pick_rows(me, ids_t, weights_t, tokens, out_grad, expert_count, capacity):
    rows, width = tokens.shape
    block = jax.ShapeDtypeStruct((2 * capacity, width), jnp.bfloat16)
    picks = pltpu.VMEM((expert_count * 2 * capacity, rows), jnp.bfloat16)
    return pl.pallas_call(
        functools.partial(pick_kernel, expert_count, capacity),
        out_shape=[block] * expert_count,
        in_specs=[smem(), vmem(), vmem(), vmem(), vmem()],
        out_specs=[vmem()] * expert_count,
        scratch_shapes=[picks, picks],
        compiler_params=params(),
        cost_estimate=cost(1e9, 4e6),
        name="pick_rows",
    )(me, ids_t, weights_t, tokens, out_grad)


NT = (((1,), (1,)), ((), ()))


def expert_kernel(capacity, count, groups, *refs):
    blocks, weights = refs[:count], refs[count : count + 6]
    parcel_ref, mine_ref = refs[count + 6 : count + 8]
    keep_refs = refs[count + 8 : count + 8 + len(groups)]
    send_refs = refs[count + 8 + len(groups) :]
    gates, ups, downs = weights[0:2], weights[2:4], weights[4:6]
    width, units = gates[0].shape
    rows = count * capacity
    tiles = chunks(width, 896)
    totals = [[jnp.zeros((rows, units), jnp.float32)] * 3 for _ in range(2)]
    for at, tile in tiles:
        here = slice(at, at + tile)
        there = slice(width + at, width + at + tile)
        for i, ref in enumerate(blocks):
            value = ref[:, here].astype(jnp.float32)
            place = slice(i * capacity, (i + 1) * capacity)
            parcel_ref[place, here] = value[:capacity].astype(jnp.bfloat16)
            parcel_ref[place, there] = value[capacity:].astype(jnp.bfloat16)
        x = parcel_ref[:, here]
        dy = parcel_ref[:, there]
        for core, total in enumerate(totals):
            total[0] += jnp.dot(x, gates[core][here, :], preferred_element_type=jnp.float32)
            total[1] += jnp.dot(x, ups[core][here, :], preferred_element_type=jnp.float32)
            total[2] += lax.dot_general(
                dy, downs[core][:, here], NT, preferred_element_type=jnp.float32
            )
    route = jnp.zeros((rows, 1), jnp.float32)
    unit_refs = (mine_ref, parcel_ref.at[:, 2 * width :])
    for (gate_value, up_value, back), out in zip(totals, unit_refs):
        sigmoid = jax.nn.sigmoid(gate_value)
        silu = gate_value * sigmoid
        hidden = (silu * up_value).astype(jnp.bfloat16)
        d_gate = back * up_value * sigmoid * (1.0 + gate_value * (1.0 - sigmoid))
        out[:, 0:units] = d_gate.astype(jnp.bfloat16)
        out[:, units : 2 * units] = (back * silu).astype(jnp.bfloat16)
        out[:, 2 * units :] = hidden
        route += jnp.sum(hidden.astype(jnp.float32) * back, axis=1, keepdims=True)

    def put(value, here):
        value = value.astype(jnp.bfloat16)
        for out_refs, at in ((keep_refs, 0), (send_refs, rows // 2)):
            for out, size in zip(out_refs, groups):
                out[:, here] = value[at : at + size * capacity]
                at += size * capacity

    put(jnp.broadcast_to(route, (rows, EXTRA)), slice(width, width + EXTRA))
    for at, tile in tiles:
        here = slice(at, at + tile)
        part = jnp.zeros((rows, tile), jnp.float32)
        for core, out in enumerate(unit_refs):
            part += lax.dot_general(
                out[:, 0:units], gates[core][here, :], NT, preferred_element_type=jnp.float32
            )
            part += lax.dot_general(
                out[:, units : 2 * units],
                ups[core][here, :],
                NT,
                preferred_element_type=jnp.float32,
            )
        put(part, here)


def run_expert(blocks, weights, capacity, groups):
    width = blocks[0].shape[1]
    units = weights[0].shape[1]
    count = len(blocks)
    rows = count * capacity
    outs = [jax.ShapeDtypeStruct((size * capacity, width + EXTRA), jnp.bfloat16) for size in groups]
    unit_rows = jax.ShapeDtypeStruct((rows, 3 * units), jnp.bfloat16)
    parcel = jax.ShapeDtypeStruct((rows, 2 * width + 3 * units), jnp.bfloat16)
    out = pl.pallas_call(
        functools.partial(expert_kernel, capacity, count, groups),
        out_shape=[parcel, unit_rows] + outs + outs,
        in_specs=[vmem()] * (count + 6),
        out_specs=[vmem()] * (2 + 2 * len(groups)),
        compiler_params=pltpu.CompilerParams(vmem_limit_bytes=EXPERT_VMEM),
        cost_estimate=cost(20 * rows * width * units, 12 * width * units + 10 * rows * width),
        name="run_expert",
    )(*blocks, *weights)
    return out[0], out[1], out[2 : 2 + len(groups)], out[2 + len(groups) :]


def finish_kernel(capacity, keep_ref, far_ref, *outs):
    half = (far_ref.shape[1] - EXTRA) // 2

    def summed(part):
        return keep_ref[:, part].astype(jnp.float32) + far_ref[:, part].astype(jnp.float32)

    for h in range(2):
        for start, size in chunks(half, 896):
            value = summed(slice(h * half + start, h * half + start + size))
            for i, out in enumerate(outs):
                out[h * capacity : (h + 1) * capacity, start : start + size] = value[
                    i * capacity : (i + 1) * capacity
                ].astype(jnp.bfloat16)
    value = summed(slice(2 * half, 2 * half + EXTRA))
    for i, out in enumerate(outs):
        block = value[i * capacity : (i + 1) * capacity].astype(jnp.bfloat16)
        out[0:capacity, half:] = block
        out[capacity:, half:] = block


def finish(keep, far, capacity):
    rows, width = far.shape
    count = rows // capacity
    half = (width - EXTRA) // 2
    block = jax.ShapeDtypeStruct((2 * capacity, half + EXTRA), jnp.bfloat16)
    return pl.pallas_call(
        functools.partial(finish_kernel, capacity),
        out_shape=[block] * count,
        in_specs=[vmem()] * 2,
        out_specs=[vmem()] * count,
        compiler_params=params(),
        cost_estimate=cost(2 * rows * width, 6 * rows * width),
        name="finish",
    )(keep, far)


def weight_kernel(group_rows, width, *refs):
    count = len(group_rows)
    parcels, unit_refs = refs[:count], refs[count : 2 * count]
    gate_ref, up_ref, down_ref, all_units = refs[2 * count :]
    tile, units = gate_ref.shape

    @pl.when(pl.program_id(0) == 0)
    def _():
        at = 0
        for rows, parcel, own in zip(group_rows, parcels, unit_refs):
            source = parcel if own is None else own
            all_units[at : at + rows, :] = source[:, source.shape[1] - 3 * units :]
            at += rows

    x_at = pl.multiple_of(pl.program_id(0) * tile, 128)
    dy_at = pl.multiple_of(width + pl.program_id(0) * tile, 128)
    x_rows = jnp.concatenate([parcel[:, pl.ds(x_at, tile)] for parcel in parcels], axis=0)
    dy_rows = jnp.concatenate([parcel[:, pl.ds(dy_at, tile)] for parcel in parcels], axis=0)
    contract = (((0,), (0,)), ((), ()))
    grads = lax.dot_general(
        x_rows, all_units[:, 0 : 2 * units], contract, preferred_element_type=jnp.float32
    )
    gate_ref[...] = grads[:, :units].astype(jnp.bfloat16)
    up_ref[...] = grads[:, units:].astype(jnp.bfloat16)
    down_ref[...] = lax.dot_general(
        all_units[:, 2 * units :], dy_rows, contract, preferred_element_type=jnp.float32
    ).astype(jnp.bfloat16)


def weight_grads(parcels, units, width):
    hidden_units = (parcels[0].shape[1] - 2 * width) // 3
    group_rows = [p.shape[0] for p in parcels]
    total = sum(group_rows)
    tile = width // 4 if width % (128 * 4) == 0 else width
    given = [own for own in units if own is not None]

    def kernel(*refs):
        rest = list(refs[len(parcels) : len(parcels) + len(given)])
        owns = [None if own is None else rest.pop(0) for own in units]
        weight_kernel(
            group_rows, width, *refs[: len(parcels)], *owns, *refs[len(parcels) + len(given) :]
        )

    return pl.pallas_call(
        kernel,
        grid=(width // tile,),
        out_shape=[
            jax.ShapeDtypeStruct((width, hidden_units), jnp.bfloat16),
            jax.ShapeDtypeStruct((width, hidden_units), jnp.bfloat16),
            jax.ShapeDtypeStruct((hidden_units, width), jnp.bfloat16),
        ],
        in_specs=[vmem()] * (len(parcels) + len(given)),
        out_specs=[
            pl.BlockSpec((tile, hidden_units), lambda i: (i, 0)),
            pl.BlockSpec((tile, hidden_units), lambda i: (i, 0)),
            pl.BlockSpec((hidden_units, tile), lambda i: (0, i)),
        ],
        scratch_shapes=[pltpu.VMEM((total, 3 * hidden_units), jnp.bfloat16)],
        compiler_params=params(),
        cost_estimate=cost(
            6 * total * width * hidden_units, 4 * total * width + 6 * width * hidden_units
        ),
        name="weight_grads",
    )(*parcels, *given)


def combine_kernel(expert_count, capacity, me_ref, ids_ref, weight_ref, *refs):
    blocks = refs[:expert_count]
    tok_ref, route_ref, slots, values = refs[expert_count:]
    routes, rows = ids_ref.shape
    half = blocks[0].shape[1] - EXTRA
    hits, slot_t = find_slots(expert_count, me_ref[0], ids_ref[...])
    slots[...] = jnp.full(slots.shape, -1.0, jnp.float32)
    slots[0:expert_count, :] = slot_t
    slot = slots[...].T.astype(jnp.int32)
    lane = lax.broadcasted_iota(jnp.int32, (rows, slots.shape[0]), 1)
    index = lax.broadcasted_iota(jnp.int32, (rows, 2 * capacity), 1)
    picks = []
    for s in range(expert_count):
        column = slot[:, s : s + 1]
        low = jnp.where(column == index, 1.0, 0.0)
        high = jnp.where((column >= 0) & (column + capacity == index), 1.0, 0.0)
        picks.append(jnp.concatenate([low, high], axis=0).astype(jnp.bfloat16))
    for start, size in chunks(half, 896):
        part = jnp.zeros((2 * rows, size), jnp.float32)
        for s in range(expert_count):
            part += jnp.dot(
                picks[s], blocks[s][:, start : start + size], preferred_element_type=jnp.float32
            )
        tok_ref[:, start : start + size] = part[:rows].astype(jnp.bfloat16)
        tok_ref[:, half + start : half + start + size] = part[rows:].astype(jnp.bfloat16)
    value = jnp.zeros((rows, slots.shape[0]), jnp.float32)
    for s in range(expert_count):
        found = jnp.dot(picks[s], blocks[s][:, half:], preferred_element_type=jnp.float32)
        value = jnp.where(lane == s, found[:rows, 0:1], value)
    values[...] = value.T
    value_t = values[0:expert_count, :]
    weights = weight_ref[...].astype(jnp.float32)
    found = [
        jnp.sum(jnp.where(hit, value_t, 0.0), axis=0, keepdims=True) for hit in hits
    ]
    route_ref[...] = (jnp.concatenate(found, axis=0) / weights).astype(jnp.bfloat16)


def combine(me, ids_t, weights_t, blocks, capacity):
    routes, rows = ids_t.shape
    half = blocks[0].shape[1] - EXTRA
    return pl.pallas_call(
        functools.partial(combine_kernel, len(blocks), capacity),
        out_shape=[
            jax.ShapeDtypeStruct((rows, 2 * half), jnp.bfloat16),
            jax.ShapeDtypeStruct((routes, rows), jnp.bfloat16),
        ],
        in_specs=[smem()] + [vmem()] * (2 + len(blocks)),
        out_specs=[vmem(), vmem()],
        scratch_shapes=[pltpu.VMEM((128, rows), jnp.float32), pltpu.VMEM((128, rows), jnp.float32)],
        compiler_params=params(),
        cost_estimate=cost(1e9, 3e6),
        name="combine",
    )(me, ids_t, weights_t, *blocks)


def source_groups(expert_count):
    half, three = expert_count // 2, 3 * expert_count // 4
    return [
        list(range(half)),
        list(range(three, expert_count)),
        list(range(half, three)),
    ]


def after(*values):
    return lax.optimization_barrier(values)


def shards(tokens, out_grad, expert_ids, route_weights, w_gate, w_up, w_down):
    expert_count = lax.axis_size("expert")
    group_count = lax.axis_size("dp")
    device_count = expert_count * group_count
    capacity = 5 * tokens.shape[0] // (4 * expert_count)
    if (2 * capacity) % 8:
        capacity = -(-capacity // 8) * 8
    me = lax.axis_index("expert").astype(jnp.int32).reshape(1)
    ids_t, weights_t = expert_ids.T, route_weights.T

    def swap(value, distance):
        return lax.ppermute(value, AXES, [(i, i ^ distance) for i in range(device_count)])

    near, first, second = source_groups(expert_count)
    got, crossed, back = {}, {}, {}

    def fetch(group, source):
        for s in group:
            got[s] = swap(source[s], s * group_count) if s else source[s]

    def cross(group):
        for s in group:
            crossed[s] = swap(got[s], 2)

    def ready(group, keep, far):
        return dict(zip(group, finish(keep, far, capacity)))

    def give(blocks):
        for s, block in blocks.items():
            back[s] = swap(block, s * group_count) if s else block

    weights = []
    for own in (w_gate[0], w_up[0], w_down[0]):
        weights += [own, swap(own, 1)]
    blocks = list(pick_rows(me, ids_t, weights_t, tokens, out_grad, expert_count, capacity))
    fetch(first, blocks)
    weights, close = after(weights, {s: blocks[s] for s in near})
    fetch(near, close)
    cross(near[:-1])
    early, waiting = {s: crossed[s] for s in near[:-2]}, {s: blocks[s] for s in second}
    got, early, weights, waiting = after(got, early, weights, waiting)
    crossed.update(early)
    fetch(second, waiting)
    cross(near[-1:] + first)
    got, crossed = after(got, crossed)
    cross(second)

    def work(*groups):
        order = sum(groups, [])
        return run_expert(
            [got[s] for s in order] + [crossed[s] for s in order],
            weights,
            capacity,
            [len(group) for group in groups],
        )

    left, right = near[: len(near) // 2], near[len(near) // 2 :]
    parcel, units, keeps, sends = work(first, left, right)
    ahead = {s: crossed[s] for s in second}
    keeps, ahead = after(keeps, ahead)
    crossed.update(ahead)
    last_parcel, last_units, last_keeps, last_sends = work(second)
    first_far = swap(sends[0], 2)
    left_far = swap(sends[1], 2)
    first_ready = ready(first, keeps[0], first_far)
    first_ready, last_sends = after(first_ready, last_sends)
    give(first_ready)
    second_far = swap(last_sends[0], 2)
    right_far = swap(sends[2], 2)
    second_ready = ready(second, last_keeps[0], second_far)
    left_ready = ready(left, keeps[1], left_far)
    returned = {s: back[s] for s in first}
    returned, left_ready, second_ready, parcel, last_parcel = after(
        returned, left_ready, second_ready, parcel, last_parcel
    )
    other = swap(parcel, 1)
    back.update(returned)
    give(second_ready)
    give(left_ready)
    last_other = swap(last_parcel, 1)
    forth = second[0]
    back[forth], right_far = after(back[forth], right_far)
    right_ready = ready(right, keeps[2], right_far)
    other, last_other, right_ready = after(other, last_other, right_ready)
    give(right_ready)
    parcels = [parcel, last_parcel, other, last_other]
    grads = weight_grads(parcels, [units, last_units, None, None], tokens.shape[1])
    grads, back = after(list(grads), back)
    grad_gate, grad_up, grad_down = grads
    grad_tokens, grad_route_t = combine(
        me, ids_t, weights_t, [back[s] for s in range(expert_count)], capacity
    )
    return (grad_tokens, grad_route_t.T, grad_gate[None], grad_up[None], grad_down[None])


def solution(mesh):
    rows = P(AXES, None)
    columns = P("expert", None, "dp")
    return jax.shard_map(
        shards,
        mesh=mesh,
        in_specs=(rows, rows, rows, rows, columns, columns, P("expert", "dp", None)),
        out_specs=(rows, rows, columns, columns, P("expert", "dp", None)),
        check_vma=False,
    )
```

```python
import functools

import jax
import jax.numpy as jnp
from jax import lax
from jax.experimental import pallas as pl
from jax.experimental.pallas import tpu as pltpu
from jax.sharding import PartitionSpec as P

AXES = ("expert", "dp")
VMEM_LIMIT = 24 * 1024 * 1024
EXTRA = 128
EXPERT_VMEM = 24 * 1024 * 1024


def vmem():
    return pl.BlockSpec(memory_space=pltpu.VMEM)


def smem():
    return pl.BlockSpec(memory_space=pltpu.SMEM)


def params():
    return pltpu.CompilerParams(vmem_limit_bytes=VMEM_LIMIT)


def cost(flops, size):
    return pl.CostEstimate(flops=int(flops), bytes_accessed=int(size), transcendentals=0)


def chunks(total, step):
    return [(start, min(step, total - start)) for start in range(0, total, step)]


def find_slots(expert_count, me, ids_t):
    rows = ids_t.shape[1]
    target = lax.broadcasted_iota(jnp.int32, (expert_count, rows), 0) ^ me
    hits = [ids_t[k : k + 1, :] == target for k in range(ids_t.shape[0])]
    has = functools.reduce(jnp.logical_or, hits)
    before = lax.broadcasted_iota(jnp.int32, (rows, rows), 0) < lax.broadcasted_iota(
        jnp.int32, (rows, rows), 1
    )
    rank = jnp.dot(
        has.astype(jnp.float32).astype(jnp.bfloat16),
        before.astype(jnp.float32).astype(jnp.bfloat16),
        preferred_element_type=jnp.float32,
    )
    return hits, jnp.where(has, rank, -1.0)


def pick_kernel(expert_count, capacity, me_ref, ids_ref, weight_ref, tok_ref, grad_ref, *refs):
    outs, pick_x, pick_dy = refs[:expert_count], refs[expert_count], refs[expert_count + 1]
    rows, width = tok_ref.shape
    hits, slot_f = find_slots(expert_count, me_ref[0], ids_ref[...])
    weights = weight_ref[...].astype(jnp.float32)
    weight = jnp.zeros((expert_count, rows), jnp.float32)
    for k, hit in enumerate(hits):
        weight = jnp.where(hit, weights[k : k + 1, :], weight)
    slot = slot_f.astype(jnp.int32)
    block = 2 * capacity
    index = lax.broadcasted_iota(jnp.int32, (block, rows), 0)
    for s in range(expert_count):
        mine = slot[s : s + 1, :]
        place = slice(s * block, (s + 1) * block)
        pick_x[place, :] = jnp.where(mine == index, 1.0, 0.0).astype(jnp.bfloat16)
        taken = (mine >= 0) & (mine + capacity == index)
        pick_dy[place, :] = jnp.where(taken, weight[s : s + 1, :], 0.0).astype(jnp.bfloat16)
    for start, size in chunks(width, 512):
        part = slice(start, start + size)
        picked = jnp.dot(pick_x[...], tok_ref[:, part], preferred_element_type=jnp.float32)
        picked += jnp.dot(pick_dy[...], grad_ref[:, part], preferred_element_type=jnp.float32)
        picked = picked.astype(jnp.bfloat16)
        for s in range(expert_count):
            outs[s][:, part] = picked[s * block : (s + 1) * block]


def pick_rows(me, ids_t, weights_t, tokens, out_grad, expert_count, capacity):
    rows, width = tokens.shape
    block = jax.ShapeDtypeStruct((2 * capacity, width), jnp.bfloat16)
    picks = pltpu.VMEM((expert_count * 2 * capacity, rows), jnp.bfloat16)
    return pl.pallas_call(
        functools.partial(pick_kernel, expert_count, capacity),
        out_shape=[block] * expert_count,
        in_specs=[smem(), vmem(), vmem(), vmem(), vmem()],
        out_specs=[vmem()] * expert_count,
        scratch_shapes=[picks, picks],
        compiler_params=params(),
        cost_estimate=cost(1e9, 4e6),
        name="pick_rows",
    )(me, ids_t, weights_t, tokens, out_grad)


NT = (((1,), (1,)), ((), ()))


def expert_kernel(capacity, count, groups, *refs):
    blocks, weights = refs[:count], refs[count : count + 6]
    parcel_ref, mine_ref = refs[count + 6 : count + 8]
    keep_refs = refs[count + 8 : count + 8 + len(groups)]
    send_refs = refs[count + 8 + len(groups) :]
    gates, ups, downs = weights[0:2], weights[2:4], weights[4:6]
    width, units = gates[0].shape
    rows = count * capacity
    tiles = chunks(width, 896)
    totals = [[jnp.zeros((rows, units), jnp.float32)] * 3 for _ in range(2)]
    for at, tile in tiles:
        here = slice(at, at + tile)
        there = slice(width + at, width + at + tile)
        for i, ref in enumerate(blocks):
            value = ref[:, here].astype(jnp.float32)
            place = slice(i * capacity, (i + 1) * capacity)
            parcel_ref[place, here] = value[:capacity].astype(jnp.bfloat16)
            parcel_ref[place, there] = value[capacity:].astype(jnp.bfloat16)
        x = parcel_ref[:, here]
        dy = parcel_ref[:, there]
        for core, total in enumerate(totals):
            total[0] += jnp.dot(x, gates[core][here, :], preferred_element_type=jnp.float32)
            total[1] += jnp.dot(x, ups[core][here, :], preferred_element_type=jnp.float32)
            total[2] += lax.dot_general(
                dy, downs[core][:, here], NT, preferred_element_type=jnp.float32
            )
    route = jnp.zeros((rows, 1), jnp.float32)
    unit_refs = (mine_ref, parcel_ref.at[:, 2 * width :])
    for (gate_value, up_value, back), out in zip(totals, unit_refs):
        sigmoid = jax.nn.sigmoid(gate_value)
        silu = gate_value * sigmoid
        hidden = (silu * up_value).astype(jnp.bfloat16)
        d_gate = back * up_value * sigmoid * (1.0 + gate_value * (1.0 - sigmoid))
        out[:, 0:units] = d_gate.astype(jnp.bfloat16)
        out[:, units : 2 * units] = (back * silu).astype(jnp.bfloat16)
        out[:, 2 * units :] = hidden
        route += jnp.sum(hidden.astype(jnp.float32) * back, axis=1, keepdims=True)

    def put(value, here):
        value = value.astype(jnp.bfloat16)
        for out_refs, at in ((keep_refs, 0), (send_refs, rows // 2)):
            for out, size in zip(out_refs, groups):
                out[:, here] = value[at : at + size * capacity]
                at += size * capacity

    put(jnp.broadcast_to(route, (rows, EXTRA)), slice(width, width + EXTRA))
    for at, tile in tiles:
        here = slice(at, at + tile)
        part = jnp.zeros((rows, tile), jnp.float32)
        for core, out in enumerate(unit_refs):
            part += lax.dot_general(
                out[:, 0:units], gates[core][here, :], NT, preferred_element_type=jnp.float32
            )
            part += lax.dot_general(
                out[:, units : 2 * units],
                ups[core][here, :],
                NT,
                preferred_element_type=jnp.float32,
            )
        put(part, here)


def run_expert(blocks, weights, capacity, groups):
    width = blocks[0].shape[1]
    units = weights[0].shape[1]
    count = len(blocks)
    rows = count * capacity
    outs = [jax.ShapeDtypeStruct((size * capacity, width + EXTRA), jnp.bfloat16) for size in groups]
    unit_rows = jax.ShapeDtypeStruct((rows, 3 * units), jnp.bfloat16)
    parcel = jax.ShapeDtypeStruct((rows, 2 * width + 3 * units), jnp.bfloat16)
    out = pl.pallas_call(
        functools.partial(expert_kernel, capacity, count, groups),
        out_shape=[parcel, unit_rows] + outs + outs,
        in_specs=[vmem()] * (count + 6),
        out_specs=[vmem()] * (2 + 2 * len(groups)),
        compiler_params=pltpu.CompilerParams(vmem_limit_bytes=EXPERT_VMEM),
        cost_estimate=cost(20 * rows * width * units, 12 * width * units + 10 * rows * width),
        name="run_expert",
    )(*blocks, *weights)
    return out[0], out[1], out[2 : 2 + len(groups)], out[2 + len(groups) :]


def finish_kernel(capacity, keep_ref, far_ref, *outs):
    half = (far_ref.shape[1] - EXTRA) // 2

    def summed(part):
        return keep_ref[:, part].astype(jnp.float32) + far_ref[:, part].astype(jnp.float32)

    for h in range(2):
        for start, size in chunks(half, 896):
            value = summed(slice(h * half + start, h * half + start + size))
            for i, out in enumerate(outs):
                out[h * capacity : (h + 1) * capacity, start : start + size] = value[
                    i * capacity : (i + 1) * capacity
                ].astype(jnp.bfloat16)
    value = summed(slice(2 * half, 2 * half + EXTRA))
    for i, out in enumerate(outs):
        block = value[i * capacity : (i + 1) * capacity].astype(jnp.bfloat16)
        out[0:capacity, half:] = block
        out[capacity:, half:] = block


def finish(keep, far, capacity):
    rows, width = far.shape
    count = rows // capacity
    half = (width - EXTRA) // 2
    block = jax.ShapeDtypeStruct((2 * capacity, half + EXTRA), jnp.bfloat16)
    return pl.pallas_call(
        functools.partial(finish_kernel, capacity),
        out_shape=[block] * count,
        in_specs=[vmem()] * 2,
        out_specs=[vmem()] * count,
        compiler_params=params(),
        cost_estimate=cost(2 * rows * width, 6 * rows * width),
        name="finish",
    )(keep, far)


def weight_kernel(group_rows, width, *refs):
    count = len(group_rows)
    parcels, unit_refs = refs[:count], refs[count : 2 * count]
    gate_ref, up_ref, down_ref, all_units = refs[2 * count :]
    tile, units = gate_ref.shape

    @pl.when(pl.program_id(0) == 0)
    def _():
        at = 0
        for rows, parcel, own in zip(group_rows, parcels, unit_refs):
            source = parcel if own is None else own
            all_units[at : at + rows, :] = source[:, source.shape[1] - 3 * units :]
            at += rows

    x_at = pl.multiple_of(pl.program_id(0) * tile, 128)
    dy_at = pl.multiple_of(width + pl.program_id(0) * tile, 128)
    x_rows = jnp.concatenate([parcel[:, pl.ds(x_at, tile)] for parcel in parcels], axis=0)
    dy_rows = jnp.concatenate([parcel[:, pl.ds(dy_at, tile)] for parcel in parcels], axis=0)
    contract = (((0,), (0,)), ((), ()))
    grads = lax.dot_general(
        x_rows, all_units[:, 0 : 2 * units], contract, preferred_element_type=jnp.float32
    )
    gate_ref[...] = grads[:, :units].astype(jnp.bfloat16)
    up_ref[...] = grads[:, units:].astype(jnp.bfloat16)
    down_ref[...] = lax.dot_general(
        all_units[:, 2 * units :], dy_rows, contract, preferred_element_type=jnp.float32
    ).astype(jnp.bfloat16)


def weight_grads(parcels, units, width):
    hidden_units = (parcels[0].shape[1] - 2 * width) // 3
    group_rows = [p.shape[0] for p in parcels]
    total = sum(group_rows)
    tile = width // 4 if width % (128 * 4) == 0 else width
    given = [own for own in units if own is not None]

    def kernel(*refs):
        rest = list(refs[len(parcels) : len(parcels) + len(given)])
        owns = [None if own is None else rest.pop(0) for own in units]
        weight_kernel(
            group_rows, width, *refs[: len(parcels)], *owns, *refs[len(parcels) + len(given) :]
        )

    return pl.pallas_call(
        kernel,
        grid=(width // tile,),
        out_shape=[
            jax.ShapeDtypeStruct((width, hidden_units), jnp.bfloat16),
            jax.ShapeDtypeStruct((width, hidden_units), jnp.bfloat16),
            jax.ShapeDtypeStruct((hidden_units, width), jnp.bfloat16),
        ],
        in_specs=[vmem()] * (len(parcels) + len(given)),
        out_specs=[
            pl.BlockSpec((tile, hidden_units), lambda i: (i, 0)),
            pl.BlockSpec((tile, hidden_units), lambda i: (i, 0)),
            pl.BlockSpec((hidden_units, tile), lambda i: (0, i)),
        ],
        scratch_shapes=[pltpu.VMEM((total, 3 * hidden_units), jnp.bfloat16)],
        compiler_params=params(),
        cost_estimate=cost(
            6 * total * width * hidden_units, 4 * total * width + 6 * width * hidden_units
        ),
        name="weight_grads",
    )(*parcels, *given)


def combine_kernel(expert_count, capacity, me_ref, ids_ref, weight_ref, *refs):
    blocks = refs[:expert_count]
    tok_ref, route_ref, slots, values = refs[expert_count:]
    routes, rows = ids_ref.shape
    half = blocks[0].shape[1] - EXTRA
    hits, slot_t = find_slots(expert_count, me_ref[0], ids_ref[...])
    slots[...] = jnp.full(slots.shape, -1.0, jnp.float32)
    slots[0:expert_count, :] = slot_t
    block = 2 * capacity
    columns = expert_count * block
    column = lax.broadcasted_iota(jnp.int32, (slots.shape[0], columns), 1)
    source = lax.broadcasted_iota(jnp.int32, (slots.shape[0], columns), 0)
    spread = (column >= source * block) & (column < (source + 1) * block)
    spread = spread.astype(jnp.float32).astype(jnp.bfloat16)
    slot = jnp.dot(slots[...].T.astype(jnp.bfloat16), spread, preferred_element_type=jnp.float32)
    index = (lax.broadcasted_iota(jnp.int32, (rows, columns), 1) % block).astype(jnp.float32)
    low = jnp.where(slot == index, 1.0, 0.0)
    high = jnp.where((slot >= 0.0) & (slot + capacity == index), 1.0, 0.0)
    picks = jnp.concatenate([low, high], axis=0).astype(jnp.bfloat16)
    for start, size in chunks(half, 896):
        rows_in = jnp.concatenate([ref[:, start : start + size] for ref in blocks], axis=0)
        part = jnp.dot(picks, rows_in, preferred_element_type=jnp.float32)
        tok_ref[:, start : start + size] = part[:rows].astype(jnp.bfloat16)
        tok_ref[:, half + start : half + start + size] = part[rows:].astype(jnp.bfloat16)
    lane = lax.broadcasted_iota(jnp.int32, (block, slots.shape[0]), 1)
    apart = [
        jnp.where(lane == s, ref[:, half:].astype(jnp.float32), 0.0).astype(jnp.bfloat16)
        for s, ref in enumerate(blocks)
    ]
    value = jnp.dot(
        picks[:rows], jnp.concatenate(apart, axis=0), preferred_element_type=jnp.float32
    )
    values[...] = value.T
    value_t = values[0:expert_count, :]
    weights = weight_ref[...].astype(jnp.float32)
    found = [
        jnp.sum(jnp.where(hit, value_t, 0.0), axis=0, keepdims=True) for hit in hits
    ]
    route_ref[...] = (jnp.concatenate(found, axis=0) / weights).astype(jnp.bfloat16)


def combine(me, ids_t, weights_t, blocks, capacity):
    routes, rows = ids_t.shape
    half = blocks[0].shape[1] - EXTRA
    return pl.pallas_call(
        functools.partial(combine_kernel, len(blocks), capacity),
        out_shape=[
            jax.ShapeDtypeStruct((rows, 2 * half), jnp.bfloat16),
            jax.ShapeDtypeStruct((routes, rows), jnp.bfloat16),
        ],
        in_specs=[smem()] + [vmem()] * (2 + len(blocks)),
        out_specs=[vmem(), vmem()],
        scratch_shapes=[pltpu.VMEM((128, rows), jnp.float32), pltpu.VMEM((128, rows), jnp.float32)],
        compiler_params=params(),
        cost_estimate=cost(1e9, 3e6),
        name="combine",
    )(me, ids_t, weights_t, *blocks)


def source_groups(expert_count):
    half, three = expert_count // 2, 3 * expert_count // 4
    return [
        list(range(half)),
        list(range(three, expert_count)),
        list(range(half, three)),
    ]


def after(*values):
    return lax.optimization_barrier(values)


def shards(tokens, out_grad, expert_ids, route_weights, w_gate, w_up, w_down):
    expert_count = lax.axis_size("expert")
    group_count = lax.axis_size("dp")
    device_count = expert_count * group_count
    capacity = 5 * tokens.shape[0] // (4 * expert_count)
    if (2 * capacity) % 8:
        capacity = -(-capacity // 8) * 8
    me = lax.axis_index("expert").astype(jnp.int32).reshape(1)
    ids_t, weights_t = expert_ids.T, route_weights.T

    def swap(value, distance):
        return lax.ppermute(value, AXES, [(i, i ^ distance) for i in range(device_count)])

    near, first, second = source_groups(expert_count)
    got, crossed, back = {}, {}, {}

    def fetch(group, source):
        for s in group:
            got[s] = swap(source[s], s * group_count) if s else source[s]

    def cross(group):
        for s in group:
            crossed[s] = swap(got[s], 2)

    def ready(group, keep, far):
        return dict(zip(group, finish(keep, far, capacity)))

    def give(blocks):
        for s, block in blocks.items():
            back[s] = swap(block, s * group_count) if s else block

    weights = []
    for own in (w_gate[0], w_up[0], w_down[0]):
        weights += [own, swap(own, 1)]
    blocks = list(pick_rows(me, ids_t, weights_t, tokens, out_grad, expert_count, capacity))
    fetch(first, blocks)
    weights, close = after(weights, {s: blocks[s] for s in near})
    fetch(near, close)
    cross(near[:-1])
    early, waiting = {s: crossed[s] for s in near[:-2]}, {s: blocks[s] for s in second}
    got, early, weights, waiting = after(got, early, weights, waiting)
    crossed.update(early)
    fetch(second, waiting)
    cross(near[-1:] + first)
    got, crossed = after(got, crossed)
    cross(second)

    def work(*groups):
        order = sum(groups, [])
        return run_expert(
            [got[s] for s in order] + [crossed[s] for s in order],
            weights,
            capacity,
            [len(group) for group in groups],
        )

    left, right = near[: len(near) // 2], near[len(near) // 2 :]
    parcel, units, keeps, sends = work(first, left, right)
    ahead = {s: crossed[s] for s in second}
    keeps, ahead = after(keeps, ahead)
    crossed.update(ahead)
    last_parcel, last_units, last_keeps, last_sends = work(second)
    first_far = swap(sends[0], 2)
    left_far = swap(sends[1], 2)
    first_ready = ready(first, keeps[0], first_far)
    first_ready, last_sends = after(first_ready, last_sends)
    give(first_ready)
    second_far = swap(last_sends[0], 2)
    right_far = swap(sends[2], 2)
    second_ready = ready(second, last_keeps[0], second_far)
    left_ready = ready(left, keeps[1], left_far)
    returned = {s: back[s] for s in first}
    returned, left_ready, second_ready, parcel, last_parcel = after(
        returned, left_ready, second_ready, parcel, last_parcel
    )
    other = swap(parcel, 1)
    back.update(returned)
    give(second_ready)
    give(left_ready)
    last_other = swap(last_parcel, 1)
    forth = second[0]
    back[forth], right_far = after(back[forth], right_far)
    right_ready = ready(right, keeps[2], right_far)
    other, last_other, right_ready = after(other, last_other, right_ready)
    give(right_ready)
    parcels = [parcel, last_parcel, other, last_other]
    grads = weight_grads(parcels, [units, last_units, None, None], tokens.shape[1])
    grad_gate, grad_up, grad_down = grads
    grad_tokens, grad_route_t = combine(
        me, ids_t, weights_t, [back[s] for s in range(expert_count)], capacity
    )
    return (grad_tokens, grad_route_t.T, grad_gate[None], grad_up[None], grad_down[None])


def solution(mesh):
    rows = P(AXES, None)
    columns = P("expert", None, "dp")
    return jax.shard_map(
        shards,
        mesh=mesh,
        in_specs=(rows, rows, rows, rows, columns, columns, P("expert", "dp", None)),
        out_specs=(rows, rows, columns, columns, P("expert", "dp", None)),
        check_vma=False,
    )
```

```python
import functools

import jax
import jax.numpy as jnp
from jax import lax
from jax.experimental import pallas as pl
from jax.experimental.pallas import tpu as pltpu
from jax.sharding import PartitionSpec as P

AXES = ("expert", "dp")
VMEM_LIMIT = 24 * 1024 * 1024
EXTRA = 128
EXPERT_VMEM = 24 * 1024 * 1024


def vmem():
    return pl.BlockSpec(memory_space=pltpu.VMEM)


def smem():
    return pl.BlockSpec(memory_space=pltpu.SMEM)


def params():
    return pltpu.CompilerParams(vmem_limit_bytes=VMEM_LIMIT)


def cost(flops, size):
    return pl.CostEstimate(flops=int(flops), bytes_accessed=int(size), transcendentals=0)


def chunks(total, step):
    return [(start, min(step, total - start)) for start in range(0, total, step)]


def find_slots(expert_count, me, ids_t):
    rows = ids_t.shape[1]
    target = lax.broadcasted_iota(jnp.int32, (expert_count, rows), 0) ^ me
    hits = [ids_t[k : k + 1, :] == target for k in range(ids_t.shape[0])]
    has = functools.reduce(jnp.logical_or, hits)
    before = lax.broadcasted_iota(jnp.int32, (rows, rows), 0) < lax.broadcasted_iota(
        jnp.int32, (rows, rows), 1
    )
    rank = jnp.dot(
        has.astype(jnp.float32).astype(jnp.bfloat16),
        before.astype(jnp.float32).astype(jnp.bfloat16),
        preferred_element_type=jnp.float32,
    )
    return hits, jnp.where(has, rank, -1.0)


def pick_kernel(expert_count, capacity, me_ref, ids_ref, weight_ref, tok_ref, grad_ref, *refs):
    outs, pick_x, pick_dy = refs[:expert_count], refs[expert_count], refs[expert_count + 1]
    rows, width = tok_ref.shape
    hits, slot_f = find_slots(expert_count, me_ref[0], ids_ref[...])
    weights = weight_ref[...].astype(jnp.float32)
    weight = jnp.zeros((expert_count, rows), jnp.float32)
    for k, hit in enumerate(hits):
        weight = jnp.where(hit, weights[k : k + 1, :], weight)
    slot = slot_f.astype(jnp.int32)
    block = 2 * capacity
    index = lax.broadcasted_iota(jnp.int32, (block, rows), 0)
    for s in range(expert_count):
        mine = slot[s : s + 1, :]
        place = slice(s * block, (s + 1) * block)
        pick_x[place, :] = jnp.where(mine == index, 1.0, 0.0).astype(jnp.bfloat16)
        taken = (mine >= 0) & (mine + capacity == index)
        pick_dy[place, :] = jnp.where(taken, weight[s : s + 1, :], 0.0).astype(jnp.bfloat16)
    for start, size in chunks(width, 512):
        part = slice(start, start + size)
        picked = jnp.dot(pick_x[...], tok_ref[:, part], preferred_element_type=jnp.float32)
        picked += jnp.dot(pick_dy[...], grad_ref[:, part], preferred_element_type=jnp.float32)
        picked = picked.astype(jnp.bfloat16)
        for s in range(expert_count):
            outs[s][:, part] = picked[s * block : (s + 1) * block]


def pick_rows(me, ids_t, weights_t, tokens, out_grad, expert_count, capacity):
    rows, width = tokens.shape
    block = jax.ShapeDtypeStruct((2 * capacity, width), jnp.bfloat16)
    picks = pltpu.VMEM((expert_count * 2 * capacity, rows), jnp.bfloat16)
    return pl.pallas_call(
        functools.partial(pick_kernel, expert_count, capacity),
        out_shape=[block] * expert_count,
        in_specs=[smem(), vmem(), vmem(), vmem(), vmem()],
        out_specs=[vmem()] * expert_count,
        scratch_shapes=[picks, picks],
        compiler_params=params(),
        cost_estimate=cost(1e9, 4e6),
        name="pick_rows",
    )(me, ids_t, weights_t, tokens, out_grad)


NT = (((1,), (1,)), ((), ()))


def expert_kernel(capacity, count, groups, *refs):
    blocks, weights = refs[:count], refs[count : count + 6]
    parcel_ref, mine_ref = refs[count + 6 : count + 8]
    keep_refs = refs[count + 8 : count + 8 + len(groups)]
    send_refs = refs[count + 8 + len(groups) :]
    gates, ups, downs = weights[0:2], weights[2:4], weights[4:6]
    width, units = gates[0].shape
    rows = count * capacity
    tiles = chunks(width, 896)
    totals = [[jnp.zeros((rows, units), jnp.float32)] * 3 for _ in range(2)]
    for at, tile in tiles:
        here = slice(at, at + tile)
        there = slice(width + at, width + at + tile)
        for i, ref in enumerate(blocks):
            value = ref[:, here].astype(jnp.float32)
            place = slice(i * capacity, (i + 1) * capacity)
            parcel_ref[place, here] = value[:capacity].astype(jnp.bfloat16)
            parcel_ref[place, there] = value[capacity:].astype(jnp.bfloat16)
        x = parcel_ref[:, here]
        dy = parcel_ref[:, there]
        for core, total in enumerate(totals):
            total[0] += jnp.dot(x, gates[core][here, :], preferred_element_type=jnp.float32)
            total[1] += jnp.dot(x, ups[core][here, :], preferred_element_type=jnp.float32)
            total[2] += lax.dot_general(
                dy, downs[core][:, here], NT, preferred_element_type=jnp.float32
            )
    route = jnp.zeros((rows, 1), jnp.float32)
    unit_refs = (mine_ref, parcel_ref.at[:, 2 * width :])
    for (gate_value, up_value, back), out in zip(totals, unit_refs):
        sigmoid = jax.nn.sigmoid(gate_value)
        silu = gate_value * sigmoid
        hidden = (silu * up_value).astype(jnp.bfloat16)
        d_gate = back * up_value * sigmoid * (1.0 + gate_value * (1.0 - sigmoid))
        out[:, 0:units] = d_gate.astype(jnp.bfloat16)
        out[:, units : 2 * units] = (back * silu).astype(jnp.bfloat16)
        out[:, 2 * units :] = hidden
        route += jnp.sum(hidden.astype(jnp.float32) * back, axis=1, keepdims=True)

    def put(value, here):
        value = value.astype(jnp.bfloat16)
        for out_refs, at in ((keep_refs, 0), (send_refs, rows // 2)):
            for out, size in zip(out_refs, groups):
                out[:, here] = value[at : at + size * capacity]
                at += size * capacity

    put(jnp.broadcast_to(route, (rows, EXTRA)), slice(width, width + EXTRA))
    for at, tile in tiles:
        here = slice(at, at + tile)
        part = jnp.zeros((rows, tile), jnp.float32)
        for core, out in enumerate(unit_refs):
            part += lax.dot_general(
                out[:, 0:units], gates[core][here, :], NT, preferred_element_type=jnp.float32
            )
            part += lax.dot_general(
                out[:, units : 2 * units],
                ups[core][here, :],
                NT,
                preferred_element_type=jnp.float32,
            )
        put(part, here)


def run_expert(blocks, weights, capacity, groups):
    width = blocks[0].shape[1]
    units = weights[0].shape[1]
    count = len(blocks)
    rows = count * capacity
    outs = [jax.ShapeDtypeStruct((size * capacity, width + EXTRA), jnp.bfloat16) for size in groups]
    unit_rows = jax.ShapeDtypeStruct((rows, 3 * units), jnp.bfloat16)
    parcel = jax.ShapeDtypeStruct((rows, 2 * width + 3 * units), jnp.bfloat16)
    out = pl.pallas_call(
        functools.partial(expert_kernel, capacity, count, groups),
        out_shape=[parcel, unit_rows] + outs + outs,
        in_specs=[vmem()] * (count + 6),
        out_specs=[vmem()] * (2 + 2 * len(groups)),
        compiler_params=pltpu.CompilerParams(vmem_limit_bytes=EXPERT_VMEM),
        cost_estimate=cost(20 * rows * width * units, 12 * width * units + 10 * rows * width),
        name="run_expert",
    )(*blocks, *weights)
    return out[0], out[1], out[2 : 2 + len(groups)], out[2 + len(groups) :]


def finish_kernel(capacity, keep_ref, far_ref, *outs):
    half = (far_ref.shape[1] - EXTRA) // 2

    def summed(part):
        return keep_ref[:, part].astype(jnp.float32) + far_ref[:, part].astype(jnp.float32)

    for h in range(2):
        for start, size in chunks(half, 896):
            value = summed(slice(h * half + start, h * half + start + size))
            for i, out in enumerate(outs):
                out[h * capacity : (h + 1) * capacity, start : start + size] = value[
                    i * capacity : (i + 1) * capacity
                ].astype(jnp.bfloat16)
    value = summed(slice(2 * half, 2 * half + EXTRA))
    for i, out in enumerate(outs):
        block = value[i * capacity : (i + 1) * capacity].astype(jnp.bfloat16)
        out[0:capacity, half:] = block
        out[capacity:, half:] = block


def finish(keep, far, capacity):
    rows, width = far.shape
    count = rows // capacity
    half = (width - EXTRA) // 2
    block = jax.ShapeDtypeStruct((2 * capacity, half + EXTRA), jnp.bfloat16)
    return pl.pallas_call(
        functools.partial(finish_kernel, capacity),
        out_shape=[block] * count,
        in_specs=[vmem()] * 2,
        out_specs=[vmem()] * count,
        compiler_params=params(),
        cost_estimate=cost(2 * rows * width, 6 * rows * width),
        name="finish",
    )(keep, far)


def weight_kernel(group_rows, width, *refs):
    count = len(group_rows)
    parcels, unit_refs = refs[:count], refs[count : 2 * count]
    gate_ref, up_ref, down_ref, all_units = refs[2 * count :]
    tile, units = gate_ref.shape

    @pl.when(pl.program_id(0) == 0)
    def _():
        at = 0
        for rows, parcel, own in zip(group_rows, parcels, unit_refs):
            source = parcel if own is None else own
            all_units[at : at + rows, :] = source[:, source.shape[1] - 3 * units :]
            at += rows

    x_at = pl.multiple_of(pl.program_id(0) * tile, 128)
    dy_at = pl.multiple_of(width + pl.program_id(0) * tile, 128)
    x_rows = jnp.concatenate([parcel[:, pl.ds(x_at, tile)] for parcel in parcels], axis=0)
    dy_rows = jnp.concatenate([parcel[:, pl.ds(dy_at, tile)] for parcel in parcels], axis=0)
    contract = (((0,), (0,)), ((), ()))
    grads = lax.dot_general(
        x_rows, all_units[:, 0 : 2 * units], contract, preferred_element_type=jnp.float32
    )
    gate_ref[...] = grads[:, :units].astype(jnp.bfloat16)
    up_ref[...] = grads[:, units:].astype(jnp.bfloat16)
    down_ref[...] = lax.dot_general(
        all_units[:, 2 * units :], dy_rows, contract, preferred_element_type=jnp.float32
    ).astype(jnp.bfloat16)


def weight_grads(parcels, units, width):
    hidden_units = (parcels[0].shape[1] - 2 * width) // 3
    group_rows = [p.shape[0] for p in parcels]
    total = sum(group_rows)
    tile = width // 4 if width % (128 * 4) == 0 else width
    given = [own for own in units if own is not None]

    def kernel(*refs):
        rest = list(refs[len(parcels) : len(parcels) + len(given)])
        owns = [None if own is None else rest.pop(0) for own in units]
        weight_kernel(
            group_rows, width, *refs[: len(parcels)], *owns, *refs[len(parcels) + len(given) :]
        )

    return pl.pallas_call(
        kernel,
        grid=(width // tile,),
        out_shape=[
            jax.ShapeDtypeStruct((width, hidden_units), jnp.bfloat16),
            jax.ShapeDtypeStruct((width, hidden_units), jnp.bfloat16),
            jax.ShapeDtypeStruct((hidden_units, width), jnp.bfloat16),
        ],
        in_specs=[vmem()] * (len(parcels) + len(given)),
        out_specs=[
            pl.BlockSpec((tile, hidden_units), lambda i: (i, 0)),
            pl.BlockSpec((tile, hidden_units), lambda i: (i, 0)),
            pl.BlockSpec((hidden_units, tile), lambda i: (0, i)),
        ],
        scratch_shapes=[pltpu.VMEM((total, 3 * hidden_units), jnp.bfloat16)],
        compiler_params=params(),
        cost_estimate=cost(
            6 * total * width * hidden_units, 4 * total * width + 6 * width * hidden_units
        ),
        name="weight_grads",
    )(*parcels, *given)


def combine_kernel(expert_count, capacity, me_ref, ids_ref, weight_ref, *refs):
    blocks = refs[:expert_count]
    tok_ref, route_ref, slots, values = refs[expert_count:]
    routes, rows = ids_ref.shape
    half = blocks[0].shape[1] - EXTRA
    hits, slot_t = find_slots(expert_count, me_ref[0], ids_ref[...])
    slots[...] = jnp.full(slots.shape, -1.0, jnp.float32)
    slots[0:expert_count, :] = slot_t
    block = 2 * capacity
    columns = expert_count * block
    column = lax.broadcasted_iota(jnp.int32, (slots.shape[0], columns), 1)
    source = lax.broadcasted_iota(jnp.int32, (slots.shape[0], columns), 0)
    spread = (column >= source * block) & (column < (source + 1) * block)
    spread = spread.astype(jnp.float32).astype(jnp.bfloat16)
    slot = jnp.dot(slots[...].T.astype(jnp.bfloat16), spread, preferred_element_type=jnp.float32)
    index = (lax.broadcasted_iota(jnp.int32, (rows, columns), 1) % block).astype(jnp.float32)
    low = jnp.where(slot == index, 1.0, 0.0)
    high = jnp.where((slot >= 0.0) & (slot + capacity == index), 1.0, 0.0)
    picks = jnp.concatenate([low, high], axis=0).astype(jnp.bfloat16)
    for start, size in chunks(half, 896):
        rows_in = jnp.concatenate([ref[:, start : start + size] for ref in blocks], axis=0)
        part = jnp.dot(picks, rows_in, preferred_element_type=jnp.float32)
        tok_ref[:, start : start + size] = part[:rows].astype(jnp.bfloat16)
        tok_ref[:, half + start : half + start + size] = part[rows:].astype(jnp.bfloat16)
    lane = lax.broadcasted_iota(jnp.int32, (block, slots.shape[0]), 1)
    apart = [
        jnp.where(lane == s, ref[:, half:].astype(jnp.float32), 0.0).astype(jnp.bfloat16)
        for s, ref in enumerate(blocks)
    ]
    value = jnp.dot(
        picks[:rows], jnp.concatenate(apart, axis=0), preferred_element_type=jnp.float32
    )
    values[...] = value.T
    value_t = values[0:expert_count, :]
    weights = weight_ref[...].astype(jnp.float32)
    found = [
        jnp.sum(jnp.where(hit, value_t, 0.0), axis=0, keepdims=True) for hit in hits
    ]
    route_ref[...] = (jnp.concatenate(found, axis=0) / weights).astype(jnp.bfloat16)


def combine(me, ids_t, weights_t, blocks, capacity):
    routes, rows = ids_t.shape
    half = blocks[0].shape[1] - EXTRA
    return pl.pallas_call(
        functools.partial(combine_kernel, len(blocks), capacity),
        out_shape=[
            jax.ShapeDtypeStruct((rows, 2 * half), jnp.bfloat16),
            jax.ShapeDtypeStruct((routes, rows), jnp.bfloat16),
        ],
        in_specs=[smem()] + [vmem()] * (2 + len(blocks)),
        out_specs=[vmem(), vmem()],
        scratch_shapes=[pltpu.VMEM((128, rows), jnp.float32), pltpu.VMEM((128, rows), jnp.float32)],
        compiler_params=params(),
        cost_estimate=cost(1e9, 3e6),
        name="combine",
    )(me, ids_t, weights_t, *blocks)


def source_groups(expert_count):
    half, three = expert_count // 2, 3 * expert_count // 4
    return [
        list(range(half)),
        list(range(three, expert_count)),
        list(range(half, three)),
    ]


def after(*values):
    return lax.optimization_barrier(values)


def shards(tokens, out_grad, expert_ids, route_weights, w_gate, w_up, w_down):
    expert_count = lax.axis_size("expert")
    group_count = lax.axis_size("dp")
    device_count = expert_count * group_count
    capacity = 5 * tokens.shape[0] // (4 * expert_count)
    if (2 * capacity) % 8:
        capacity = -(-capacity // 8) * 8
    me = lax.axis_index("expert").astype(jnp.int32).reshape(1)
    ids_t, weights_t = expert_ids.T, route_weights.T

    def swap(value, distance):
        return lax.ppermute(value, AXES, [(i, i ^ distance) for i in range(device_count)])

    near, first, second = source_groups(expert_count)
    got, crossed, back = {}, {}, {}

    def fetch(group, source):
        for s in group:
            got[s] = swap(source[s], s * group_count) if s else source[s]

    def cross(group):
        for s in group:
            crossed[s] = swap(got[s], 2)

    def ready(group, keep, far):
        return dict(zip(group, finish(keep, far, capacity)))

    def give(blocks):
        for s, block in blocks.items():
            back[s] = swap(block, s * group_count) if s else block

    weights = []
    for own in (w_gate[0], w_up[0], w_down[0]):
        weights += [own, swap(own, 1)]
    blocks = list(pick_rows(me, ids_t, weights_t, tokens, out_grad, expert_count, capacity))
    fetch(first, blocks)
    fetch(near[:2], blocks)
    weights, close = after(weights, {s: blocks[s] for s in near[2:-1]})
    fetch(near[2:-1], close)
    cross(near[:-1])
    early, waiting = {s: crossed[s] for s in near[:-2]}, {s: blocks[s] for s in second + near[-1:]}
    got, early, weights, waiting = after(got, early, weights, waiting)
    crossed.update(early)
    fetch(second + near[-1:], waiting)
    cross(first[:1])
    queue = first[1:] + near[-1:]
    for before, s in zip([first[0], near[-2]] + queue, queue):
        crossed[before], got[s] = after(crossed[before], got[s])
        cross([s])
    got, crossed = after(got, crossed)
    cross(second)

    def work(*groups):
        order = sum(groups, [])
        return run_expert(
            [got[s] for s in order] + [crossed[s] for s in order],
            weights,
            capacity,
            [len(group) for group in groups],
        )

    right, left = near[: len(near) // 2], near[len(near) // 2 :]
    parcel, units, keeps, sends = work(first, left, right)
    ahead = {s: crossed[s] for s in second}
    keeps, ahead = after(keeps, ahead)
    crossed.update(ahead)
    last_parcel, last_units, last_keeps, last_sends = work(second)
    first_far = swap(sends[0], 2)
    left_far = swap(sends[1], 2)
    first_ready = ready(first, keeps[0], first_far)
    first_ready, last_sends = after(first_ready, last_sends)
    give(first_ready)
    second_far = swap(last_sends[0], 2)
    right_far = swap(sends[2], 2)
    second_ready = ready(second, last_keeps[0], second_far)
    left_ready = ready(left, keeps[1], left_far)
    returned = {s: back[s] for s in first}
    returned, left_ready, second_ready, parcel, last_parcel = after(
        returned, left_ready, second_ready, parcel, last_parcel
    )
    other = swap(parcel, 1)
    back.update(returned)
    give(second_ready)
    give(left_ready)
    last_other = swap(last_parcel, 1)
    forth = second[0]
    back[forth], right_far = after(back[forth], right_far)
    right_ready = ready(right, keeps[2], right_far)
    other, last_other, right_ready = after(other, last_other, right_ready)
    give(right_ready)
    parcels = [parcel, last_parcel, other, last_other]
    grads = weight_grads(parcels, [units, last_units, None, None], tokens.shape[1])
    grad_gate, grad_up, grad_down = grads
    grad_tokens, grad_route_t = combine(
        me, ids_t, weights_t, [back[s] for s in range(expert_count)], capacity
    )
    return (grad_tokens, grad_route_t.T, grad_gate[None], grad_up[None], grad_down[None])


def solution(mesh):
    rows = P(AXES, None)
    columns = P("expert", None, "dp")
    return jax.shard_map(
        shards,
        mesh=mesh,
        in_specs=(rows, rows, rows, rows, columns, columns, P("expert", "dp", None)),
        out_specs=(rows, rows, columns, columns, P("expert", "dp", None)),
        check_vma=False,
    )
```

```python
import functools

import jax
import jax.numpy as jnp
from jax import lax
from jax.experimental import pallas as pl
from jax.experimental.pallas import tpu as pltpu
from jax.sharding import PartitionSpec as P

AXES = ("expert", "dp")
VMEM_LIMIT = 24 * 1024 * 1024
EXTRA = 128
EXPERT_VMEM = 24 * 1024 * 1024


def vmem():
    return pl.BlockSpec(memory_space=pltpu.VMEM)


def smem():
    return pl.BlockSpec(memory_space=pltpu.SMEM)


def params():
    return pltpu.CompilerParams(vmem_limit_bytes=VMEM_LIMIT)


def cost(flops, size):
    return pl.CostEstimate(flops=int(flops), bytes_accessed=int(size), transcendentals=0)


def chunks(total, step):
    return [(start, min(step, total - start)) for start in range(0, total, step)]


def find_slots(expert_count, me, ids_t):
    rows = ids_t.shape[1]
    target = lax.broadcasted_iota(jnp.int32, (expert_count, rows), 0) ^ me
    hits = [ids_t[k : k + 1, :] == target for k in range(ids_t.shape[0])]
    has = functools.reduce(jnp.logical_or, hits)
    before = lax.broadcasted_iota(jnp.int32, (rows, rows), 0) < lax.broadcasted_iota(
        jnp.int32, (rows, rows), 1
    )
    rank = jnp.dot(
        has.astype(jnp.float32).astype(jnp.bfloat16),
        before.astype(jnp.float32).astype(jnp.bfloat16),
        preferred_element_type=jnp.float32,
    )
    return hits, jnp.where(has, rank, -1.0)


def pick_kernel(expert_count, capacity, me_ref, ids_ref, weight_ref, tok_ref, grad_ref, *refs):
    outs, pick_x, pick_dy = refs[:expert_count], refs[expert_count], refs[expert_count + 1]
    rows, width = tok_ref.shape
    hits, slot_f = find_slots(expert_count, me_ref[0], ids_ref[...])
    weights = weight_ref[...].astype(jnp.float32)
    weight = jnp.zeros((expert_count, rows), jnp.float32)
    for k, hit in enumerate(hits):
        weight = jnp.where(hit, weights[k : k + 1, :], weight)
    slot = slot_f.astype(jnp.int32)
    block = 2 * capacity
    index = lax.broadcasted_iota(jnp.int32, (block, rows), 0)
    for s in range(expert_count):
        mine = slot[s : s + 1, :]
        place = slice(s * block, (s + 1) * block)
        pick_x[place, :] = jnp.where(mine == index, 1.0, 0.0).astype(jnp.bfloat16)
        taken = (mine >= 0) & (mine + capacity == index)
        pick_dy[place, :] = jnp.where(taken, weight[s : s + 1, :], 0.0).astype(jnp.bfloat16)
    for start, size in chunks(width, 512):
        part = slice(start, start + size)
        picked = jnp.dot(pick_x[...], tok_ref[:, part], preferred_element_type=jnp.float32)
        picked += jnp.dot(pick_dy[...], grad_ref[:, part], preferred_element_type=jnp.float32)
        picked = picked.astype(jnp.bfloat16)
        for s in range(expert_count):
            outs[s][:, part] = picked[s * block : (s + 1) * block]


def pick_rows(me, ids_t, weights_t, tokens, out_grad, expert_count, capacity):
    rows, width = tokens.shape
    block = jax.ShapeDtypeStruct((2 * capacity, width), jnp.bfloat16)
    picks = pltpu.VMEM((expert_count * 2 * capacity, rows), jnp.bfloat16)
    return pl.pallas_call(
        functools.partial(pick_kernel, expert_count, capacity),
        out_shape=[block] * expert_count,
        in_specs=[smem(), vmem(), vmem(), vmem(), vmem()],
        out_specs=[vmem()] * expert_count,
        scratch_shapes=[picks, picks],
        compiler_params=params(),
        cost_estimate=cost(1e9, 4e6),
        name="pick_rows",
    )(me, ids_t, weights_t, tokens, out_grad)


NT = (((1,), (1,)), ((), ()))


def expert_kernel(capacity, count, groups, *refs):
    blocks, weights = refs[:count], refs[count : count + 6]
    parcel_ref, mine_ref = refs[count + 6 : count + 8]
    keep_refs = refs[count + 8 : count + 8 + len(groups)]
    send_refs = refs[count + 8 + len(groups) :]
    gates, ups, downs = weights[0:2], weights[2:4], weights[4:6]
    width, units = gates[0].shape
    rows = count * capacity
    tiles = chunks(width, 896)
    totals = [[jnp.zeros((rows, units), jnp.float32)] * 3 for _ in range(2)]
    for at, tile in tiles:
        here = slice(at, at + tile)
        there = slice(width + at, width + at + tile)
        for i, ref in enumerate(blocks):
            value = ref[:, here].astype(jnp.float32)
            place = slice(i * capacity, (i + 1) * capacity)
            parcel_ref[place, here] = value[:capacity].astype(jnp.bfloat16)
            parcel_ref[place, there] = value[capacity:].astype(jnp.bfloat16)
        x = parcel_ref[:, here]
        dy = parcel_ref[:, there]
        for core, total in enumerate(totals):
            total[0] += jnp.dot(x, gates[core][here, :], preferred_element_type=jnp.float32)
            total[1] += jnp.dot(x, ups[core][here, :], preferred_element_type=jnp.float32)
            total[2] += lax.dot_general(
                dy, downs[core][:, here], NT, preferred_element_type=jnp.float32
            )
    route = jnp.zeros((rows, 1), jnp.float32)
    unit_refs = (mine_ref, parcel_ref.at[:, 2 * width :])
    for (gate_value, up_value, back), out in zip(totals, unit_refs):
        sigmoid = jax.nn.sigmoid(gate_value)
        silu = gate_value * sigmoid
        hidden = (silu * up_value).astype(jnp.bfloat16)
        d_gate = back * up_value * sigmoid * (1.0 + gate_value * (1.0 - sigmoid))
        out[:, 0:units] = d_gate.astype(jnp.bfloat16)
        out[:, units : 2 * units] = (back * silu).astype(jnp.bfloat16)
        out[:, 2 * units :] = hidden
        route += jnp.sum(hidden.astype(jnp.float32) * back, axis=1, keepdims=True)

    def put(value, here):
        value = value.astype(jnp.bfloat16)
        for out_refs, at in ((keep_refs, 0), (send_refs, rows // 2)):
            for out, size in zip(out_refs, groups):
                out[:, here] = value[at : at + size * capacity]
                at += size * capacity

    put(jnp.broadcast_to(route, (rows, EXTRA)), slice(width, width + EXTRA))
    for at, tile in tiles:
        here = slice(at, at + tile)
        part = jnp.zeros((rows, tile), jnp.float32)
        for core, out in enumerate(unit_refs):
            part += lax.dot_general(
                out[:, 0:units], gates[core][here, :], NT, preferred_element_type=jnp.float32
            )
            part += lax.dot_general(
                out[:, units : 2 * units],
                ups[core][here, :],
                NT,
                preferred_element_type=jnp.float32,
            )
        put(part, here)


def run_expert(blocks, weights, capacity, groups):
    width = blocks[0].shape[1]
    units = weights[0].shape[1]
    count = len(blocks)
    rows = count * capacity
    outs = [jax.ShapeDtypeStruct((size * capacity, width + EXTRA), jnp.bfloat16) for size in groups]
    unit_rows = jax.ShapeDtypeStruct((rows, 3 * units), jnp.bfloat16)
    parcel = jax.ShapeDtypeStruct((rows, 2 * width + 3 * units), jnp.bfloat16)
    out = pl.pallas_call(
        functools.partial(expert_kernel, capacity, count, groups),
        out_shape=[parcel, unit_rows] + outs + outs,
        in_specs=[vmem()] * (count + 6),
        out_specs=[vmem()] * (2 + 2 * len(groups)),
        compiler_params=pltpu.CompilerParams(vmem_limit_bytes=EXPERT_VMEM),
        cost_estimate=cost(20 * rows * width * units, 12 * width * units + 10 * rows * width),
        name="run_expert",
    )(*blocks, *weights)
    return out[0], out[1], out[2 : 2 + len(groups)], out[2 + len(groups) :]


def finish_kernel(capacity, keep_ref, far_ref, *outs):
    half = (far_ref.shape[1] - EXTRA) // 2

    def summed(part):
        return keep_ref[:, part].astype(jnp.float32) + far_ref[:, part].astype(jnp.float32)

    for h in range(2):
        for start, size in chunks(half, 896):
            value = summed(slice(h * half + start, h * half + start + size))
            for i, out in enumerate(outs):
                out[h * capacity : (h + 1) * capacity, start : start + size] = value[
                    i * capacity : (i + 1) * capacity
                ].astype(jnp.bfloat16)
    value = summed(slice(2 * half, 2 * half + EXTRA))
    for i, out in enumerate(outs):
        block = value[i * capacity : (i + 1) * capacity].astype(jnp.bfloat16)
        out[0:capacity, half:] = block
        out[capacity:, half:] = block


def finish(keep, far, capacity):
    rows, width = far.shape
    count = rows // capacity
    half = (width - EXTRA) // 2
    block = jax.ShapeDtypeStruct((2 * capacity, half + EXTRA), jnp.bfloat16)
    return pl.pallas_call(
        functools.partial(finish_kernel, capacity),
        out_shape=[block] * count,
        in_specs=[vmem()] * 2,
        out_specs=[vmem()] * count,
        compiler_params=params(),
        cost_estimate=cost(2 * rows * width, 6 * rows * width),
        name="finish",
    )(keep, far)


def weight_kernel(group_rows, width, *refs):
    count = len(group_rows)
    parcels, unit_refs = refs[:count], refs[count : 2 * count]
    gate_ref, up_ref, down_ref, all_units = refs[2 * count :]
    tile, units = gate_ref.shape

    @pl.when(pl.program_id(0) == 0)
    def _():
        at = 0
        for rows, parcel, own in zip(group_rows, parcels, unit_refs):
            source = parcel if own is None else own
            all_units[at : at + rows, :] = source[:, source.shape[1] - 3 * units :]
            at += rows

    x_at = pl.multiple_of(pl.program_id(0) * tile, 128)
    dy_at = pl.multiple_of(width + pl.program_id(0) * tile, 128)
    x_rows = jnp.concatenate([parcel[:, pl.ds(x_at, tile)] for parcel in parcels], axis=0)
    dy_rows = jnp.concatenate([parcel[:, pl.ds(dy_at, tile)] for parcel in parcels], axis=0)
    contract = (((0,), (0,)), ((), ()))
    grads = lax.dot_general(
        x_rows, all_units[:, 0 : 2 * units], contract, preferred_element_type=jnp.float32
    )
    gate_ref[...] = grads[:, :units].astype(jnp.bfloat16)
    up_ref[...] = grads[:, units:].astype(jnp.bfloat16)
    down_ref[...] = lax.dot_general(
        all_units[:, 2 * units :], dy_rows, contract, preferred_element_type=jnp.float32
    ).astype(jnp.bfloat16)


def weight_grads(parcels, units, width):
    hidden_units = (parcels[0].shape[1] - 2 * width) // 3
    group_rows = [p.shape[0] for p in parcels]
    total = sum(group_rows)
    tile = width // 2 if width % (128 * 2) == 0 else width
    given = [own for own in units if own is not None]

    def kernel(*refs):
        rest = list(refs[len(parcels) : len(parcels) + len(given)])
        owns = [None if own is None else rest.pop(0) for own in units]
        weight_kernel(
            group_rows, width, *refs[: len(parcels)], *owns, *refs[len(parcels) + len(given) :]
        )

    return pl.pallas_call(
        kernel,
        grid=(width // tile,),
        out_shape=[
            jax.ShapeDtypeStruct((width, hidden_units), jnp.bfloat16),
            jax.ShapeDtypeStruct((width, hidden_units), jnp.bfloat16),
            jax.ShapeDtypeStruct((hidden_units, width), jnp.bfloat16),
        ],
        in_specs=[vmem()] * (len(parcels) + len(given)),
        out_specs=[
            pl.BlockSpec((tile, hidden_units), lambda i: (i, 0)),
            pl.BlockSpec((tile, hidden_units), lambda i: (i, 0)),
            pl.BlockSpec((hidden_units, tile), lambda i: (0, i)),
        ],
        scratch_shapes=[pltpu.VMEM((total, 3 * hidden_units), jnp.bfloat16)],
        compiler_params=params(),
        cost_estimate=cost(
            6 * total * width * hidden_units, 4 * total * width + 6 * width * hidden_units
        ),
        name="weight_grads",
    )(*parcels, *given)


def combine_kernel(expert_count, capacity, me_ref, ids_ref, weight_ref, *refs):
    blocks = refs[:expert_count]
    tok_ref, route_ref, slots, values = refs[expert_count:]
    routes, rows = ids_ref.shape
    half = blocks[0].shape[1] - EXTRA
    hits, slot_t = find_slots(expert_count, me_ref[0], ids_ref[...])
    slots[...] = jnp.full(slots.shape, -1.0, jnp.float32)
    slots[0:expert_count, :] = slot_t
    block = 2 * capacity
    columns = expert_count * block
    column = lax.broadcasted_iota(jnp.int32, (slots.shape[0], columns), 1)
    source = lax.broadcasted_iota(jnp.int32, (slots.shape[0], columns), 0)
    spread = (column >= source * block) & (column < (source + 1) * block)
    spread = spread.astype(jnp.float32).astype(jnp.bfloat16)
    slot = jnp.dot(slots[...].T.astype(jnp.bfloat16), spread, preferred_element_type=jnp.float32)
    index = (lax.broadcasted_iota(jnp.int32, (rows, columns), 1) % block).astype(jnp.float32)
    low = jnp.where(slot == index, 1.0, 0.0)
    high = jnp.where((slot >= 0.0) & (slot + capacity == index), 1.0, 0.0)
    picks = jnp.concatenate([low, high], axis=0).astype(jnp.bfloat16)
    for start, size in chunks(half, 896):
        rows_in = jnp.concatenate([ref[:, start : start + size] for ref in blocks], axis=0)
        part = jnp.dot(picks, rows_in, preferred_element_type=jnp.float32)
        tok_ref[:, start : start + size] = part[:rows].astype(jnp.bfloat16)
        tok_ref[:, half + start : half + start + size] = part[rows:].astype(jnp.bfloat16)
    lane = lax.broadcasted_iota(jnp.int32, (block, slots.shape[0]), 1)
    apart = [
        jnp.where(lane == s, ref[:, half:].astype(jnp.float32), 0.0).astype(jnp.bfloat16)
        for s, ref in enumerate(blocks)
    ]
    value = jnp.dot(
        picks[:rows], jnp.concatenate(apart, axis=0), preferred_element_type=jnp.float32
    )
    values[...] = value.T
    value_t = values[0:expert_count, :]
    weights = weight_ref[...].astype(jnp.float32)
    found = [
        jnp.sum(jnp.where(hit, value_t, 0.0), axis=0, keepdims=True) for hit in hits
    ]
    route_ref[...] = (jnp.concatenate(found, axis=0) / weights).astype(jnp.bfloat16)


def combine(me, ids_t, weights_t, blocks, capacity):
    routes, rows = ids_t.shape
    half = blocks[0].shape[1] - EXTRA
    return pl.pallas_call(
        functools.partial(combine_kernel, len(blocks), capacity),
        out_shape=[
            jax.ShapeDtypeStruct((rows, 2 * half), jnp.bfloat16),
            jax.ShapeDtypeStruct((routes, rows), jnp.bfloat16),
        ],
        in_specs=[smem()] + [vmem()] * (2 + len(blocks)),
        out_specs=[vmem(), vmem()],
        scratch_shapes=[pltpu.VMEM((128, rows), jnp.float32), pltpu.VMEM((128, rows), jnp.float32)],
        compiler_params=params(),
        cost_estimate=cost(1e9, 3e6),
        name="combine",
    )(me, ids_t, weights_t, *blocks)


def source_groups(expert_count):
    half, three = expert_count // 2, 3 * expert_count // 4
    return [
        list(range(half)),
        list(range(three, expert_count)),
        list(range(half, three)),
    ]


def after(*values):
    return lax.optimization_barrier(values)


def shards(tokens, out_grad, expert_ids, route_weights, w_gate, w_up, w_down):
    expert_count = lax.axis_size("expert")
    group_count = lax.axis_size("dp")
    device_count = expert_count * group_count
    capacity = 5 * tokens.shape[0] // (4 * expert_count)
    if (2 * capacity) % 8:
        capacity = -(-capacity // 8) * 8
    me = lax.axis_index("expert").astype(jnp.int32).reshape(1)
    ids_t, weights_t = expert_ids.T, route_weights.T

    def swap(value, distance):
        return lax.ppermute(value, AXES, [(i, i ^ distance) for i in range(device_count)])

    near, first, second = source_groups(expert_count)
    got, crossed, back = {}, {}, {}

    def fetch(group, source):
        for s in group:
            got[s] = swap(source[s], s * group_count) if s else source[s]

    def cross(group):
        for s in group:
            crossed[s] = swap(got[s], 2)

    def ready(group, keep, far):
        return dict(zip(group, finish(keep, far, capacity)))

    def give(blocks):
        for s, block in blocks.items():
            back[s] = swap(block, s * group_count) if s else block

    weights = []
    for own in (w_gate[0], w_up[0], w_down[0]):
        weights += [own, swap(own, 1)]
    blocks = list(pick_rows(me, ids_t, weights_t, tokens, out_grad, expert_count, capacity))
    fetch(first, blocks)
    fetch(near[:2], blocks)
    weights, close = after(weights, {s: blocks[s] for s in near[2:-1]})
    fetch(near[2:-1], close)
    cross(near[:-1])
    early, waiting = {s: crossed[s] for s in near[:-2]}, {s: blocks[s] for s in second + near[-1:]}
    got, early, weights, waiting = after(got, early, weights, waiting)
    crossed.update(early)
    fetch(second + near[-1:], waiting)
    cross(first[:1])
    queue = first[1:] + near[-1:]
    for before, s in zip([first[0], near[-2]] + queue, queue):
        crossed[before], got[s] = after(crossed[before], got[s])
        cross([s])
    got, crossed = after(got, crossed)
    cross(second)

    def work(*groups):
        order = sum(groups, [])
        return run_expert(
            [got[s] for s in order] + [crossed[s] for s in order],
            weights,
            capacity,
            [len(group) for group in groups],
        )

    right, left = near[: len(near) // 2], near[len(near) // 2 :]
    parcel, units, keeps, sends = work(first, left, right)
    ahead = {s: crossed[s] for s in second}
    keeps, ahead = after(keeps, ahead)
    crossed.update(ahead)
    last_parcel, last_units, last_keeps, last_sends = work(second)
    first_far = swap(sends[0], 2)
    left_far = swap(sends[1], 2)
    first_ready = ready(first, keeps[0], first_far)
    first_ready, last_sends = after(first_ready, last_sends)
    give(first_ready)
    second_far = swap(last_sends[0], 2)
    right_far = swap(sends[2], 2)
    second_ready = ready(second, last_keeps[0], second_far)
    left_ready = ready(left, keeps[1], left_far)
    returned = {s: back[s] for s in first}
    returned, left_ready, second_ready, parcel, last_parcel = after(
        returned, left_ready, second_ready, parcel, last_parcel
    )
    other = swap(parcel, 1)
    back.update(returned)
    give(second_ready)
    give(left_ready)
    last_other = swap(last_parcel, 1)
    forth = second[0]
    back[forth], right_far = after(back[forth], right_far)
    right_ready = ready(right, keeps[2], right_far)
    other, last_other, right_ready = after(other, last_other, right_ready)
    give(right_ready)
    parcels = [parcel, last_parcel, other, last_other]
    grads = weight_grads(parcels, [units, last_units, None, None], tokens.shape[1])
    grad_gate, grad_up, grad_down = grads
    grad_tokens, grad_route_t = combine(
        me, ids_t, weights_t, [back[s] for s in range(expert_count)], capacity
    )
    return (grad_tokens, grad_route_t.T, grad_gate[None], grad_up[None], grad_down[None])


def solution(mesh):
    rows = P(AXES, None)
    columns = P("expert", None, "dp")
    return jax.shard_map(
        shards,
        mesh=mesh,
        in_specs=(rows, rows, rows, rows, columns, columns, P("expert", "dp", None)),
        out_specs=(rows, rows, columns, columns, P("expert", "dp", None)),
        check_vma=False,
    )
```
